256 devices in a mesh: ctx: 32 (over x, z), head: 8 (over y, core).
Axes of the slice: x: 4, y: 4, z: 8, core: 2. Of those that a mesh axis runs over, the one named last changes fastest.
Arguments:
- ssm_input: bfloat16 [8192, 8192], P('ctx', 'head'), may hold values from -6 to 6
- gate_input: bfloat16 [8192, 8192], P('ctx', 'head'), may hold values from -6 to 6
- in_state: bfloat16 [8192, 1024], P('ctx', 'head'), may hold values from -0.5 to 0.5
- out_state: bfloat16 [8192, 1024], P('ctx', 'head'), may hold values from -0.5 to 0.5
- step_size: float32 [8192, 128], P('ctx', 'head'), may hold values from 0.05 to 0.5
- log_decay: float32 [8192, 128], P('ctx', 'head'), may hold values from 0 to 2
- skip_gain: float32 [128], P('head'), may hold values from 0.5 to 1.5
- norm_gain: float32 [8192], P('head'), may hold values from 0.5 to 1.5
- queries: bfloat16 [8192, 8192], P('ctx', 'head'), may hold values from -5 to 5
- keys: bfloat16 [8192, 1024], P('ctx', 'head'), may hold values from -5 to 5
- values: bfloat16 [8192, 1024], P('ctx', 'head'), may hold values from -6 to 6
Outputs:
- mamba_out: bfloat16 [8192, 8192], P('ctx', 'head')
- attention_out: bfloat16 [8192, 8192], P('ctx', 'head')
The draws below stay inside these ranges and needn't reach their ends.
All inputs are finite; a program needn't handle non-finite values.
Results may differ from the reference program's by a relative error of at most 0.014.
Values may be sent and summed in bfloat16 or wider, within the bound.
No kernel may reach another device: no remote copies, remote signals or barrier semaphores. Data moves between devices by JAX's collectives and lax.ppermute only.
A program may use at most 128 MiB of HBM per device.

```python
import math
import jax
import jax.numpy as jnp
from jax import lax

MIXER_HEADS = 128
P_SIZE = 64
N = 128
GROUPS = 8
HQ = 64
KVH = 8
DH = 128
BLOCK = 256
TOKEN_COUNT = 8192


def draw_log_decay(key, part):
    key = jax.random.fold_in(key, 11)
    segment_list = jax.random.split(key, 7)
    order = jax.random.permutation(segment_list[0], MIXER_HEADS)
    fast = order < MIXER_HEADS // 2
    fast_rate = jnp.exp(jax.random.uniform(segment_list[1], (MIXER_HEADS,), jnp.float32, jnp.log(1.0 / 50.0), jnp.log(1.0 / 30.0)))
    slow_rate = jnp.exp(jax.random.uniform(segment_list[2], (MIXER_HEADS,), jnp.float32, jnp.log(0.1 / TOKEN_COUNT), jnp.log(0.5 / TOKEN_COUNT)))
    decay_rate = jnp.where(fast, fast_rate, slow_rate)
    blocks = TOKEN_COUNT // BLOCK
    block_decay_factor = jnp.exp(jax.random.uniform(segment_list[3], (blocks, 1, MIXER_HEADS), jnp.float32, jnp.log(0.5), jnp.log(2.0)))
    block_decay_factor = jnp.broadcast_to(block_decay_factor, (blocks, BLOCK, MIXER_HEADS)).reshape(TOKEN_COUNT, MIXER_HEADS)
    token_decay_factor = jax.random.uniform(segment_list[4], (TOKEN_COUNT, MIXER_HEADS), jnp.float32, 0.5, 1.5)
    spike_position = jax.random.randint(segment_list[5], (3,), 0, TOKEN_COUNT)
    spike_magnitude = jax.random.uniform(segment_list[6], (3, MIXER_HEADS), jnp.float32, 0.22, 0.5)
    spike_matches = (jnp.arange(TOKEN_COUNT)[:, None] == spike_position[None, :]).astype(jnp.float32)
    spike_events = jnp.sum(spike_matches[:, :, None] * spike_magnitude[None], axis=1)
    return decay_rate[None, :] * block_decay_factor * token_decay_factor + spike_events


def draw_queries(key, part):
    key = jax.random.fold_in(key, 21)
    per_kv = HQ // KVH
    base = jnp.clip(jax.random.normal(key, (TOKEN_COUNT, KVH, per_kv, DH), jnp.float32), -5.0, 5.0)
    return base.reshape(TOKEN_COUNT, HQ * DH).astype(jnp.bfloat16)


def draw_keys(key, part):
    key = jax.random.fold_in(key, 31)
    base = jnp.clip(jax.random.normal(key, (TOKEN_COUNT, KVH, DH), jnp.float32), -5.0, 5.0)
    return base.reshape(TOKEN_COUNT, KVH * DH).astype(jnp.bfloat16)


def level_of(stream_key, extent, pieces, smallest, high):
    factor_of, own = 1.0, jax.random.fold_in(stream_key, 6)
    for axis_at, parts in pieces:
        draws = jnp.exp(jax.random.uniform(jax.random.fold_in(own, axis_at), (parts,), jnp.float32, smallest / len(pieces), high / len(pieces)))
        factor_of = factor_of * jnp.repeat(draws, extent[axis_at] // parts).reshape([-1 if axis == axis_at else 1 for axis in range(len(extent))])
    return factor_of


def normal_values(rng, extent, deviation, limit, shards=(), kind=jnp.bfloat16):
    entries = jax.random.normal(rng, extent, jnp.float32) * deviation
    if len(shards) > 0:
        entries = level_of(rng, extent, shards, -0.22, 0.18) * entries
    return jnp.clip(entries, min=-limit, max=limit).astype(kind)


def setup_inputs(seed: int = 0) -> dict:
    streams_of = jax.random.split(jax.random.key(seed), 12)
    return {
        "ssm_input": normal_values(streams_of[0], (TOKEN_COUNT, MIXER_HEADS * P_SIZE), 1.0, 6.0, ((0, 32), (1, 8))),
        "gate_input": normal_values(streams_of[1], (TOKEN_COUNT, MIXER_HEADS * P_SIZE), 1.0, 6.0, ((0, 32), (1, 8))),
        "in_state": normal_values(streams_of[2], (TOKEN_COUNT, GROUPS * N), N ** -0.5, 0.5, ((0, 32), (1, 8))),
        "out_state": normal_values(streams_of[3], (TOKEN_COUNT, GROUPS * N), N ** -0.5, 0.5, ((0, 32), (1, 8))),
        "step_size": jnp.clip(jnp.exp(math.log(0.5) - 2.3025851 * jax.random.uniform(streams_of[4], (TOKEN_COUNT, MIXER_HEADS), jnp.float32) ** level_of(streams_of[4], (TOKEN_COUNT, MIXER_HEADS), ((0, 32), (1, 8)), -0.2, 0.2)), 0.05, 0.5),
        "log_decay": draw_log_decay(jax.random.fold_in(streams_of[11], 71), 0),
        "skip_gain": jnp.clip(0.5 + 1.0 * jax.random.uniform(streams_of[6], (MIXER_HEADS,), jnp.float32) ** level_of(streams_of[6], (MIXER_HEADS,), ((0, 8),), -0.2, 0.2), 0.5, 1.5),
        "norm_gain": jnp.clip(1.0 + 0.1 * jax.random.normal(streams_of[7], (MIXER_HEADS * P_SIZE,), jnp.float32), 0.5, 1.5),
        "queries": draw_queries(jax.random.fold_in(streams_of[11], 71), 0),
        "keys": draw_keys(jax.random.fold_in(streams_of[11], 71), 0),
        "values": normal_values(streams_of[10], (TOKEN_COUNT, KVH * DH), 1.0, 6.0, ((0, 32), (1, 8))),
    }


HIGH = lax.Precision.HIGHEST

def block_segments(signal, enter, leave, step_size, decay):
    length = signal.shape[0]
    running_state = jnp.cumsum(decay, axis=0)
    scaled = signal * step_size[..., None]
    affinity = jnp.einsum('tgn,sgn->tsg', leave, enter, precision=HIGH)
    order = jnp.arange(length, dtype=jnp.int32)
    causal = (order[:, None] >= order[None, :])[:, :, None, None]
    spread = jnp.where(causal, running_state[:, None] - running_state[None, :], 0.0)
    mixing = jnp.where(causal, jnp.exp(-spread), 0.0) * affinity[..., None]
    within_block = jnp.einsum('tsgk,sgkp->tgkp', mixing, scaled, precision=HIGH)
    total_sum = running_state[-1]
    remain = jnp.exp(running_state - total_sum[None])
    state_contribution = jnp.einsum('sgn,sgkp->gknp', enter, scaled * remain[..., None], precision=HIGH)
    return (within_block, state_contribution, jnp.exp(-total_sum), running_state, total_sum)

def past_carryover(leave, running_state, state_matrix):
    return jnp.einsum('tgn,gknp->tgkp', leave, state_matrix, precision=HIGH) * jnp.exp(-running_state)[..., None]

def mamba_mixer(ssm_input, gate_input, in_state, out_state, step_size, log_decay, skip_gain, norm_gain):
    count = TOKEN_COUNT // BLOCK
    per_group = MIXER_HEADS // GROUPS
    signal = ssm_input.astype(jnp.float32).reshape(count, BLOCK, GROUPS, per_group, P_SIZE)
    enter = in_state.astype(jnp.float32).reshape(count, BLOCK, GROUPS, N)
    leave = out_state.astype(jnp.float32).reshape(count, BLOCK, GROUPS, N)
    stepped = step_size.reshape(count, BLOCK, GROUPS, per_group)
    decay = log_decay.reshape(count, BLOCK, GROUPS, per_group)
    skip_path = skip_gain.reshape(GROUPS, per_group)

    def advance(state_matrix, block_slice):
        signal_input, entry_state, leaving_state, step_length, decay_rows = block_slice
        within_block, state_contribution, fading_factor, running_state, total_sum = block_segments(signal_input, entry_state, leaving_state, step_length, decay_rows)
        mixed_output = within_block + past_carryover(leaving_state, running_state, state_matrix) + skip_path[..., None] * signal_input
        return (fading_factor[..., None, None] * state_matrix + state_contribution, mixed_output)
    start = jnp.zeros((GROUPS, per_group, N, P_SIZE), jnp.float32)
    _, mixed_output = lax.scan(advance, start, (signal, enter, leave, stepped, decay))
    mixed_output = mixed_output.reshape(TOKEN_COUNT, MIXER_HEADS * P_SIZE)
    gated = mixed_output * jax.nn.silu(gate_input.astype(jnp.float32))
    squares = lax.optimization_barrier(jnp.sum(gated * gated, axis=1))
    scale = lax.rsqrt(squares / (MIXER_HEADS * P_SIZE) + 1e-05)
    return (gated * scale[:, None] * norm_gain).astype(jnp.bfloat16)

def attention(queries, keys, values):
    per_kv = HQ // KVH
    query_all = queries.astype(jnp.float32).reshape(TOKEN_COUNT, KVH, per_kv, DH)
    key_all = keys.astype(jnp.float32).reshape(TOKEN_COUNT, KVH, DH)
    value_all = values.astype(jnp.float32).reshape(TOKEN_COUNT, KVH, DH)
    rows = 512 if TOKEN_COUNT % 512 == 0 else TOKEN_COUNT
    blocks = TOKEN_COUNT // rows
    key_pos = jnp.arange(TOKEN_COUNT, dtype=jnp.int32)
    factor = DH ** (-0.5)

    def one(index):
        group = index // blocks
        start = index % blocks * rows
        query_group = lax.dynamic_index_in_dim(query_all, group, 1, keepdims=False)
        query_rows = lax.dynamic_slice_in_dim(query_group, start, rows, 0)
        key_group = lax.dynamic_index_in_dim(key_all, group, 1, keepdims=False)
        value_group = lax.dynamic_index_in_dim(value_all, group, 1, keepdims=False)
        query_pos = start + jnp.arange(rows, dtype=jnp.int32)
        score = jnp.einsum('tqd,jd->qtj', query_rows, key_group, precision=HIGH) * factor
        mask = (key_pos[None, :] <= query_pos[:, None])[None]
        peak = lax.optimization_barrier(jnp.max(jnp.where(mask, score, -1e+30), axis=-1))
        weight = jnp.where(mask, jnp.exp(score - peak[..., None]), 0.0)
        total_sum = lax.optimization_barrier(jnp.sum(weight, axis=-1))
        rounded = weight.astype(jnp.bfloat16).astype(jnp.float32)
        summed = jnp.einsum('qtj,jd->qtd', rounded, value_group, precision=HIGH)
        result = summed / total_sum[..., None]
        return jnp.transpose(result, (1, 0, 2)).astype(jnp.bfloat16)
    outputs = lax.map(one, jnp.arange(KVH * blocks, dtype=jnp.int32))
    outputs = outputs.reshape(KVH, blocks, rows, per_kv, DH)
    outputs = jnp.transpose(outputs, (1, 2, 0, 3, 4))
    return outputs.reshape(TOKEN_COUNT, HQ * DH)

def reference(ssm_input, gate_input, in_state, out_state, step_size, log_decay, skip_gain, norm_gain, queries, keys, values):
    mamba_out = mamba_mixer(ssm_input, gate_input, in_state, out_state, step_size, log_decay, skip_gain, norm_gain)
    attention_out = attention(queries, keys, values)
    return (mamba_out, attention_out)
```

```python
import functools
import math

import jax
import jax.numpy as jnp
from jax import lax
from jax.experimental import pallas as pl
from jax.experimental.pallas import tpu as pltpu
from jax.sharding import PartitionSpec as P

MIXER_HEADS = 128
P_SIZE = 64
DH = 128
BLOCK = 256
XS = 4
ZS = 8
CTX = XS * ZS
HEADS = 16
WIDTH = HEADS * P_SIZE
LOG2E = math.log2(math.e)
SCALE = LOG2E * DH ** (-0.5)
F32 = jnp.float32
BF16 = jnp.bfloat16
HIGH = lax.Precision.HIGHEST
NT = (((1,), (1,)), ((), ()))
TN = (((0,), (0,)), ((), ()))


def dot(a, b, dims=(((1,), (0,)), ((), ())), precision=None):
    return lax.dot_general(a, b, dims, precision=precision, preferred_element_type=F32)


def halves(v):
    high = v.astype(BF16)
    return high, (v - high.astype(F32)).astype(BF16)


def spread_heads(v):
    lane = lax.broadcasted_iota(jnp.int32, (HEADS, WIDTH), 1)
    head = lax.broadcasted_iota(jnp.int32, (HEADS, WIDTH), 0)
    expand = jnp.where((lane >> 6) == head, 1.0, 0.0).astype(BF16)
    high, low = halves(v)
    return dot(high, expand) + dot(low, expand)


def local_kernel(x_ref, b_ref, c_ref, dt_ref, a_ref, skip_ref, y_ref, msg_ref, ec_ref):
    row = lax.broadcasted_iota(jnp.int32, (BLOCK, BLOCK), 0)
    col = lax.broadcasted_iota(jnp.int32, (BLOCK, BLOCK), 1)
    causal = col <= row
    a = a_ref[...]
    dt = dt_ref[...]
    cum = dot(jnp.where(causal, 1.0, 0.0), a, precision=HIGH)
    cum_rows = dot(a, jnp.where(row <= col, 1.0, 0.0), TN, precision=HIGH)
    last = cum[BLOCK - 1 :, :]
    ec_ref[...] = jnp.exp(-cum)
    x = x_ref[...].astype(F32)
    xs = (x * spread_heads(dt)).astype(BF16)
    xr = (x * spread_heads(dt * jnp.exp(cum - last))).astype(BF16)
    skip = spread_heads(jnp.broadcast_to(skip_ref[...], (8, HEADS)))[:1]
    fade = spread_heads(jnp.broadcast_to(jnp.exp(-last), (8, HEADS)))
    fade_high, fade_low = halves(fade)
    contrib = dot(b_ref[...], xr, TN).astype(BF16)
    for q in range(HEADS // 2):
        lanes = slice(q * 128, (q + 1) * 128)
        tail = jnp.concatenate([fade_high[:, lanes], fade_low[:, lanes]], axis=0)
        for r in range(4):
            msg_ref[q * 4 + r, 0:32, :] = contrib[r * 32 : (r + 1) * 32, lanes]
            msg_ref[q * 4 + r, 32:48, :] = tail
    affinity = jnp.where(causal, dot(c_ref[...], b_ref[...], NT), 0.0)
    cum2 = cum * LOG2E
    cum2_rows = cum_rows * LOG2E
    half = BLOCK // 2
    low_lane = lax.broadcasted_iota(jnp.int32, (BLOCK, 128), 1) < P_SIZE
    for q in range(HEADS // 2):
        lanes = slice(q * 128, (q + 1) * 128)
        xp = xs[:, lanes]
        parts = []
        for h in (2 * q, 2 * q + 1):
            across = cum2_rows[h : h + 1, :]
            down = cum2[:, h : h + 1]
            top = jnp.exp2(jnp.minimum(across[:, :half] - down[:half], 0.0)) * affinity[:half, :half]
            low = jnp.exp2(jnp.minimum(across - down[half:], 0.0)) * affinity[half:, :]
            parts.append(
                jnp.concatenate([dot(top.astype(BF16), xp[:half]), dot(low.astype(BF16), xp)], axis=0)
            )
        y_ref[:, lanes] = jnp.where(low_lane, parts[0], parts[1]) + skip[:, lanes] * x[:, lanes]


def scan_kernel(msg_ref, out_ref):
    state = jnp.zeros((32, 128), F32)
    for i in range(CTX):
        out_ref[i] = state.astype(BF16)
        piece = msg_ref[i].astype(F32)
        fade = piece[32:33] + piece[40:41]
        state = fade * state + piece[:32]


def gate_kernel(y_ref, c_ref, st_ref, ec_ref, z_ref, g_ref, ss_ref):
    ec = spread_heads(ec_ref[...])
    c = c_ref[...]
    total = jnp.zeros((BLOCK, 128), F32)
    for q in range(HEADS // 2):
        lanes = slice(q * 128, (q + 1) * 128)
        mixed = y_ref[:, lanes] + dot(c, st_ref[q]) * ec[:, lanes]
        z = z_ref[:, lanes].astype(F32)
        gated = mixed * (z / (1.0 + jnp.exp(-z)))
        g_ref[:, lanes] = gated
        total = total + gated * gated
    high, low = halves(total)
    ones = jnp.ones((8, 128), BF16)
    ss_ref[...] = dot(ones, high, NT) + dot(ones, low, NT)


def norm_kernel(g_ref, ss_ref, gain_ref, out_ref):
    total = dot(ss_ref[...], jnp.ones((8, 128), F32), TN, precision=HIGH)
    scale = lax.rsqrt(total * (1.0 / (MIXER_HEADS * P_SIZE)) + 1e-05)
    for q in range(HEADS // 2):
        lanes = slice(q * 128, (q + 1) * 128)
        out_ref[:, lanes] = (g_ref[:, lanes] * scale * gain_ref[:, lanes]).astype(BF16)


def attend_kernel(counts, first, last, flags, *refs):
    n = len(counts)
    q_ref, kv_refs = refs[0], refs[1 : 1 + n]
    refs = refs[1 + n :]
    if not first:
        m_in, l_in, acc_in = refs[:3]
        refs = refs[3:]
    if last:
        out_ref, m_ref, l_ref, acc_ref = refs
    else:
        m_ref, l_ref, acc_ref = refs
    if first:
        m_ref[...] = jnp.full((BLOCK, DH), -1e30, F32)
        l_ref[...] = jnp.zeros((BLOCK, DH), F32)
        acc_ref[...] = jnp.zeros((BLOCK, DH), F32)
    else:
        m_ref[...] = m_in[...]
        l_ref[...] = l_in[...]
        acc_ref[...] = acc_in[...]

    def one(kv_ref, b, diagonal):
        k = kv_ref[b, :BLOCK, :]
        v = kv_ref[b, BLOCK:, :]
        score = dot(q_ref[...], k, NT) * SCALE
        if diagonal:
            row = lax.broadcasted_iota(jnp.int32, (BLOCK, BLOCK), 0)
            col = lax.broadcasted_iota(jnp.int32, (BLOCK, BLOCK), 1)
            score = jnp.where(col <= row, score, -1e30)
        m_old = m_ref[...]
        m_new = jnp.maximum(m_old, jnp.max(score, axis=1, keepdims=True))
        weight = jnp.exp2(score - m_new[:, :1])
        shrink = jnp.exp2(m_old - m_new)
        l_ref[...] = l_ref[...] * shrink + (weight[:, :128] + weight[:, 128:])
        acc_ref[...] = acc_ref[...] * shrink + dot(weight.astype(BF16), v)
        m_ref[...] = m_new

    at = 0
    for kv_ref, count in zip(kv_refs, counts):
        for b in range(count):
            if first and at == 0:
                one(kv_ref, b, True)
            else:
                pl.when(flags[at] > 0)(functools.partial(one, kv_ref, b, False))
            at += 1
    if last:
        total = jnp.sum(l_ref[...], axis=1, keepdims=True)
        out_ref[...] = (acc_ref[...] / total).astype(BF16)


def attend(queries, kvs, flags, carry, last):
    first = carry is None
    counts = tuple(kv.shape[0] for kv in kvs)
    per_head = pl.BlockSpec((None, BLOCK, DH), lambda h, f: (h, 0, 0))
    columns = pl.BlockSpec((BLOCK, DH), lambda h, f: (0, h))
    carried = [jax.ShapeDtypeStruct((8, BLOCK, DH), F32)] * 3
    blocks = sum(counts)
    work = blocks * 8 * BLOCK * BLOCK
    kernel = functools.partial(attend_kernel, counts, first, last)
    return pl.pallas_call(
        kernel,
        grid_spec=pltpu.PrefetchScalarGridSpec(
            num_scalar_prefetch=1,
            grid=(8,),
            in_specs=[columns]
            + [pl.BlockSpec(kv.shape, lambda h, f: (0, 0, 0)) for kv in kvs]
            + ([] if first else [per_head] * 3),
            out_specs=columns if last else [per_head] * 3,
            scratch_shapes=[pltpu.VMEM((BLOCK, DH), F32)] * 3 if last else [],
        ),
        out_shape=jax.ShapeDtypeStruct((BLOCK, 8 * DH), BF16) if last else carried,
        compiler_params=pltpu.CompilerParams(vmem_limit_bytes=32 * 2**20),
        cost_estimate=pl.CostEstimate(
            flops=4 * work * DH, bytes_accessed=blocks * 2**17 + 6 * 2**20, transcendentals=work
        ),
        name="attend",
    )(flags, queries, *kvs, *(() if first else carry))


def call(kernel, outs, cost, *args):
    return pl.pallas_call(
        kernel,
        out_shape=outs,
        compiler_params=pltpu.CompilerParams(vmem_limit_bytes=48 * 2**20),
        cost_estimate=pl.CostEstimate(flops=cost, bytes_accessed=3 * 2**20, transcendentals=2**20),
    )(*args)


def z_pairs(d):
    return [(x * ZS + z, x * ZS + (z + d) % ZS) for x in range(XS) for z in range(ZS)]


def x_pairs(d):
    return [(x * ZS + z, (x + d) % XS * ZS + z) for x in range(XS) for z in range(ZS)]


def z_send(a, d):
    return lax.ppermute(a, "ctx", z_pairs(d))


def x_send(a, d):
    return lax.ppermute(a, "ctx", x_pairs(d))


def per_device(
    ssm_input,
    gate_input,
    in_state,
    out_state,
    step_size,
    log_decay,
    skip_gain,
    norm_gain,
    queries,
    keys,
    values,
):
    place = lax.axis_index("ctx")
    x, z = place // ZS, place % ZS
    rows = jnp.stack([x, (x + 3) % XS, (x + 1) % XS, (x + 2) % XS])

    def seen(d):
        return (rows * ZS + (z + d) % ZS < place).astype(jnp.int32)

    kv = jnp.concatenate([keys, values], axis=0)
    column = jnp.stack([kv, x_send(kv, 1), x_send(kv, -1), x_send(kv, 2)])

    struct = jax.ShapeDtypeStruct
    y, msg, ec = call(
        local_kernel,
        [
            struct((BLOCK, WIDTH), F32),
            struct((CTX, 48, 128), BF16),
            struct((BLOCK, HEADS), F32),
        ],
        500_000_000,
        ssm_input,
        in_state,
        out_state,
        step_size,
        log_decay,
        skip_gain.reshape(1, HEADS),
    )
    msg = lax.all_to_all(msg, "ctx", 0, 0)
    state = call(scan_kernel, struct((CTX, 32, 128), BF16), 1_000_000, msg)
    state = lax.all_to_all(state, "ctx", 0, 0).reshape(8, 128, 128)
    gated, squares = call(
        gate_kernel,
        [struct((BLOCK, WIDTH), F32), struct((8, BLOCK), F32)],
        100_000_000,
        y,
        out_state,
        state,
        ec,
        gate_input,
    )
    squares = lax.all_gather(squares[0], "head")
    mamba_out = call(
        norm_kernel,
        struct((BLOCK, WIDTH), BF16),
        10_000_000,
        gated,
        squares,
        norm_gain.reshape(1, WIDTH),
    )

    carry = attend(queries, [column], seen(0), None, False)
    right = left = column
    for step in range(1, 4):
        right, left = z_send(right, 1), z_send(left, -1)
        flags = jnp.concatenate([seen(-step), seen(step)])
        carry = attend(queries, [right, left], flags, carry, False)
    right, left = z_send(right[:2], 1), z_send(left[2:], -1)
    attention_out = attend(queries, [right, left], seen(4), carry, True)
    return mamba_out, attention_out


def solution(mesh):
    both = P("ctx", "head")
    return jax.shard_map(
        per_device,
        mesh=mesh,
        in_specs=(both,) * 6 + (P("head"), P("head")) + (both,) * 3,
        out_specs=(both, both),
        check_vma=False,
    )
```

```python
import functools
import math

import jax
import jax.numpy as jnp
from jax import lax
from jax.experimental import pallas as pl
from jax.experimental.pallas import tpu as pltpu
from jax.sharding import PartitionSpec as P

MIXER_HEADS = 128
P_SIZE = 64
DH = 128
BLOCK = 256
XS = 4
ZS = 8
CTX = XS * ZS
HEADS = 16
WIDTH = HEADS * P_SIZE
LOG2E = math.log2(math.e)
SCALE = LOG2E * DH ** (-0.5)
F32 = jnp.float32
BF16 = jnp.bfloat16
HIGH = lax.Precision.HIGHEST
NT = (((1,), (1,)), ((), ()))
TN = (((0,), (0,)), ((), ()))


def dot(a, b, dims=(((1,), (0,)), ((), ())), precision=None):
    return lax.dot_general(a, b, dims, precision=precision, preferred_element_type=F32)


def halves(v):
    high = v.astype(BF16)
    return high, (v - high.astype(F32)).astype(BF16)


def expansion():
    lane = lax.broadcasted_iota(jnp.int32, (HEADS, WIDTH), 1)
    head = lax.broadcasted_iota(jnp.int32, (HEADS, WIDTH), 0)
    return jnp.where((lane >> 6) == head, 1.0, 0.0).astype(BF16)


def spread_heads(v):
    high, low = halves(v)
    return dot(high, expansion(), TN) + dot(low, expansion(), TN)


def running(a):
    row = lax.broadcasted_iota(jnp.int32, (BLOCK, BLOCK), 0)
    col = lax.broadcasted_iota(jnp.int32, (BLOCK, BLOCK), 1)
    cum = dot(jnp.where(col <= row, 1.0, 0.0), a, NT, precision=HIGH)
    cum_rows = dot(a, jnp.where(row <= col, 1.0, 0.0), precision=HIGH)
    return cum, cum_rows


def contrib_kernel(x_ref, b_ref, dt_ref, a_ref, tok_ref, msg_ref):
    _, cum = running(a_ref[...])
    last = cum[:, BLOCK - 1 :]
    xr = x_ref[...].astype(F32) * spread_heads(dt_ref[...] * jnp.exp(cum - last))
    fade_high, fade_low = halves(spread_heads(jnp.broadcast_to(jnp.exp(-last), (HEADS, 8))))
    contrib = dot(b_ref[...], xr.astype(BF16), TN).astype(BF16)
    for q in range(HEADS // 2):
        lanes = slice(q * 128, (q + 1) * 128)
        tail = jnp.concatenate([fade_high[:, lanes], fade_low[:, lanes]], axis=0)
        for r in range(4):
            msg_ref[q * 4 + r, 0:32, :] = contrib[r * 32 : (r + 1) * 32, lanes]
            msg_ref[q * 4 + r, 32:48, :] = tail


def scan_kernel(msg_ref, tok_ref, out_ref):
    state = jnp.zeros((32, 128), F32)
    for i in range(CTX):
        out_ref[i] = state.astype(BF16)
        piece = msg_ref[i].astype(F32)
        fade = piece[32:33] + piece[40:41]
        state = fade * state + piece[:32]


def mix_kernel(
    x_ref, b_ref, c_ref, dt_ref, a_ref, z_ref, skip_ref, st_ref, tok_ref, g_ref, ss_ref
):
    row = lax.broadcasted_iota(jnp.int32, (BLOCK, BLOCK), 0)
    col = lax.broadcasted_iota(jnp.int32, (BLOCK, BLOCK), 1)
    cum, cum_rows = running(a_ref[...])
    x = x_ref[...].astype(F32)
    xs = (x * spread_heads(dt_ref[...])).astype(BF16)
    ec = spread_heads(jnp.exp(-cum_rows))
    skip = spread_heads(jnp.broadcast_to(skip_ref[...], (HEADS, 8)))[:1]
    c = c_ref[...]
    affinity = jnp.where(col <= row, dot(c, b_ref[...], NT), 0.0)
    cum2 = cum * LOG2E
    cum2_rows = cum_rows * LOG2E
    half = BLOCK // 2
    low_lane = lax.broadcasted_iota(jnp.int32, (BLOCK, 128), 1) < P_SIZE
    squares = jnp.zeros((BLOCK, 128), F32)
    for q in range(HEADS // 2):
        lanes = slice(q * 128, (q + 1) * 128)
        xp = xs[:, lanes]
        parts = []
        for h in (2 * q, 2 * q + 1):
            across = cum2_rows[h : h + 1, :]
            down = cum2[:, h : h + 1]
            top = jnp.exp2(jnp.minimum(across[:, :half] - down[:half], 0.0)) * affinity[:half, :half]
            low = jnp.exp2(jnp.minimum(across - down[half:], 0.0)) * affinity[half:, :]
            parts.append(
                jnp.concatenate([dot(top.astype(BF16), xp[:half]), dot(low.astype(BF16), xp)], axis=0)
            )
        mixed = jnp.where(low_lane, parts[0], parts[1]) + skip[:, lanes] * x[:, lanes]
        mixed = mixed + dot(c, st_ref[q]) * ec[:, lanes]
        z = z_ref[:, lanes].astype(F32)
        gated = mixed * (z / (1.0 + jnp.exp(-z)))
        g_ref[:, lanes] = gated.astype(BF16)
        squares = squares + gated * gated
    high, low = halves(squares)
    ones = jnp.ones((8, 128), BF16)
    ss_ref[...] = dot(ones, high, NT) + dot(ones, low, NT)


def norm_kernel(g_ref, one_ref, two_ref, three_ref, four_ref, gain_ref, out_ref):
    squares = one_ref[...] + two_ref[...] + three_ref[...] + four_ref[...]
    total = dot(squares, jnp.full((8, 128), 0.125, F32), TN, precision=HIGH)
    scale = lax.rsqrt(total * (1.0 / (MIXER_HEADS * P_SIZE)) + 1e-05)
    for q in range(HEADS // 2):
        lanes = slice(q * 128, (q + 1) * 128)
        out_ref[:, lanes] = (g_ref[:, lanes].astype(F32) * scale * gain_ref[:, lanes]).astype(BF16)


ROWS = 8 * BLOCK
LIMIT = 2.0**100


def keys_of(kv_ref, first, count):
    return kv_ref[pl.ds(first, count), :BLOCK, :].reshape(count * BLOCK, DH)


def values_of(kv_ref, first, count):
    return kv_ref[pl.ds(first, count), BLOCK:, :].reshape(count * BLOCK, DH)


def add_keys(qs_ref, k, v, l_ref, acc_ref, seen=None):
    lane = lax.broadcasted_iota(jnp.int32, k.shape, 1)
    ones = jnp.where(lane < 3, 1.0, 0.0).astype(BF16)
    score = dot(qs_ref[...], jnp.concatenate([k, ones], axis=1), NT)
    weights = []
    for j in range(0, k.shape[0], 128):
        weight = jnp.exp2(score[:, j : j + 128] * SCALE)
        if seen is not None:
            weight = jnp.where(seen[:, j : j + 128], weight, 0.0)
        weights.append(weight)
    l_ref[...] += sum(weights[1:], weights[0])
    acc_ref[...] += dot(jnp.concatenate([w.astype(BF16) for w in weights], axis=1), v)


def add_blocks(qs_ref, kv_ref, count, l_ref, acc_ref):
    @pl.loop(0, count // 2)
    def _(i):
        add_keys(qs_ref, keys_of(kv_ref, 2 * i, 2), values_of(kv_ref, 2 * i, 2), l_ref, acc_ref)

    @pl.when(count % 2 == 1)
    def _():
        at = count - 1
        add_keys(qs_ref, keys_of(kv_ref, at, 1), values_of(kv_ref, at, 1), l_ref, acc_ref)


def careful(qs_ref, kv_ref, count, m_ref, l_ref, acc_ref, diagonal=None):
    @pl.loop(0, 8)
    def _(h):
        rows = pl.ds(pl.multiple_of(h * BLOCK, BLOCK), BLOCK)

        def one(k, v, seen):
            score = dot(qs_ref[rows, :DH], k, NT) * SCALE
            if seen is not None:
                score = jnp.where(seen, score, -1e30)
            m_old = m_ref[rows, :]
            m_new = jnp.maximum(m_old, jnp.max(score, axis=1, keepdims=True))
            weight = jnp.exp2(score - m_new[:, :1])
            shrink = jnp.exp2(m_old - m_new)
            l_ref[rows, :] = l_ref[rows, :] * shrink + (weight[:, :128] + weight[:, 128:])
            acc_ref[rows, :] = acc_ref[rows, :] * shrink + dot(weight.astype(BF16), v)
            m_ref[rows, :] = m_new

        if diagonal is not None:
            one(*diagonal)

        @pl.loop(0, count)
        def _(b):
            one(keys_of(kv_ref, b, 1), values_of(kv_ref, b, 1), None)


def first_kernel(q_ref, own_ref, qs_ref, l_ref, acc_ref, tok_ref):
    tok_ref[...] = jnp.zeros((8, 128), F32)
    k = own_ref[:BLOCK, :]
    key = k.astype(F32)
    lane = lax.broadcasted_iota(jnp.int32, (BLOCK, DH), 1)
    for h in range(8):
        rows = slice(h * BLOCK, (h + 1) * BLOCK)
        q = q_ref[:, h * DH : (h + 1) * DH]
        qs_ref[rows, :DH] = q
        rest = -jnp.broadcast_to(jnp.sum(q.astype(F32) * key, axis=1, keepdims=True), (BLOCK, DH))
        pieces = jnp.zeros((BLOCK, DH), F32)
        for i in range(3):
            piece = rest.astype(BF16).astype(F32)
            pieces = jnp.where(lane == i, piece, pieces)
            rest = rest - piece
        qs_ref[rows, DH:] = pieces.astype(BF16)
    l_ref[...] = jnp.zeros((ROWS, DH), F32)
    acc_ref[...] = jnp.zeros((ROWS, DH), F32)
    row = lax.broadcasted_iota(jnp.int32, (ROWS, BLOCK), 0) & (BLOCK - 1)
    col = lax.broadcasted_iota(jnp.int32, (ROWS, BLOCK), 1)
    add_keys(qs_ref, k, own_ref[BLOCK:, :], l_ref, acc_ref, col <= row)


def next_kernel(n, counts_ref, qs_ref, *refs):
    kv_refs, (_, _, tok_in, l_ref, acc_ref, tok_ref) = refs[:n], refs[n:]
    tok_ref[...] = tok_in[...]
    for i, kv_ref in enumerate(kv_refs):
        add_blocks(qs_ref, kv_ref, counts_ref[i], l_ref, acc_ref)


def last_kernel(
    n, counts_ref, qs_ref, right_ref, left_ref, l_in, acc_in, tok_in, own_ref, *refs
):
    kv_refs, (out_ref, l_ref, acc_ref, m_ref, kv_ref, sem) = refs[:n], refs[n:]
    add_blocks(qs_ref, right_ref, counts_ref[n], l_ref, acc_ref)
    add_blocks(qs_ref, left_ref, counts_ref[n + 1], l_ref, acc_ref)

    @pl.when(jnp.logical_not(jnp.max(l_ref[...]) <= LIMIT))
    def _():
        l_ref[...] = jnp.zeros((ROWS, DH), F32)
        acc_ref[...] = jnp.zeros((ROWS, DH), F32)
        m_ref[...] = jnp.full((ROWS, DH), -1e30, F32)
        row = lax.broadcasted_iota(jnp.int32, (BLOCK, BLOCK), 0)
        col = lax.broadcasted_iota(jnp.int32, (BLOCK, BLOCK), 1)
        own = (own_ref[:BLOCK, :], own_ref[BLOCK:, :], col <= row)
        for i in range(n):
            copy = pltpu.make_async_copy(kv_refs[i], kv_ref, sem)
            copy.start()
            copy.wait()
            diagonal = own if i == 0 else None
            careful(qs_ref, kv_ref, counts_ref[i], m_ref, l_ref, acc_ref, diagonal)
        careful(qs_ref, right_ref, counts_ref[n], m_ref, l_ref, acc_ref)
        careful(qs_ref, left_ref, counts_ref[n + 1], m_ref, l_ref, acc_ref)

    for h in range(8):
        rows = slice(h * BLOCK, (h + 1) * BLOCK)
        total = jnp.sum(l_ref[rows, :], axis=1, keepdims=True)
        out_ref[:, h * DH : (h + 1) * DH] = (acc_ref[rows, :] / total).astype(BF16)


SUMS = pltpu.VMEM((ROWS, DH), F32)
TOKEN = jax.ShapeDtypeStruct((8, 128), F32)
SMEM = pl.BlockSpec(memory_space=pltpu.SMEM)
VMEM = pl.BlockSpec(memory_space=pltpu.VMEM)
PLAIN = pl.BlockSpec()
ANY = pl.BlockSpec(memory_space=pl.ANY)
KERNEL = pltpu.CompilerParams(vmem_limit_bytes=28 * 2**20)


def cost_of(blocks):
    work = blocks * ROWS * BLOCK
    return pl.CostEstimate(flops=4 * work * DH, bytes_accessed=2**20, transcendentals=work)


def attend_first(queries, own):
    return pl.pallas_call(
        first_kernel,
        in_specs=[PLAIN, PLAIN],
        out_specs=[VMEM] * 3 + [PLAIN],
        out_shape=[pltpu.VMEM((ROWS, 2 * DH), BF16), SUMS, SUMS, TOKEN],
        compiler_params=KERNEL,
        cost_estimate=cost_of(1),
        name="attend_first",
    )(queries, own)


def attend_next(counts, stacked, kvs, sums):
    n = len(kvs)
    return pl.pallas_call(
        functools.partial(next_kernel, n),
        in_specs=[SMEM, VMEM] + [PLAIN] * n + [VMEM] * 2 + [PLAIN],
        out_specs=[VMEM] * 2 + [PLAIN],
        out_shape=[SUMS, SUMS, TOKEN],
        input_output_aliases={n + 2: 0, n + 3: 1},
        compiler_params=KERNEL,
        cost_estimate=cost_of(sum(kv.shape[0] for kv in kvs)),
        name="attend_next",
    )(counts, stacked, *kvs, *sums)


def attend_last(counts, stacked, right, left, sums, own, kvs):
    return pl.pallas_call(
        functools.partial(last_kernel, len(kvs)),
        in_specs=[SMEM, VMEM, PLAIN, PLAIN, VMEM, VMEM, PLAIN, PLAIN] + [ANY] * len(kvs),
        out_specs=[PLAIN, VMEM, VMEM],
        out_shape=[jax.ShapeDtypeStruct((BLOCK, 8 * DH), BF16), SUMS, SUMS],
        scratch_shapes=[
            pltpu.VMEM((ROWS, DH), F32),
            pltpu.VMEM((XS, 2 * BLOCK, DH), BF16),
            pltpu.SemaphoreType.DMA,
        ],
        input_output_aliases={4: 1, 5: 2},
        compiler_params=KERNEL,
        cost_estimate=cost_of(4),
        name="attend_last",
    )(counts, stacked, right, left, *sums, own, *kvs)[0]


def column_kernel(x_ref, own_ref, one_ref, two_ref, three_ref, tok_ref, out_ref):
    x = x_ref[0]
    for d, ref in enumerate((own_ref, one_ref, two_ref, three_ref)):
        out_ref[lax.rem(x + XS - d, XS)] = ref[...]


def halve_kernel(right_ref, left_ref, low_ref, high_ref):
    low_ref[...] = right_ref[: XS // 2]
    high_ref[...] = left_ref[XS // 2 :]


def call(kernel, outs, cost, *args, limit=28):
    return pl.pallas_call(
        kernel,
        in_specs=[SMEM if arg.dtype == jnp.int32 else PLAIN for arg in args],
        out_shape=outs,
        compiler_params=pltpu.CompilerParams(vmem_limit_bytes=limit * 2**20),
        cost_estimate=pl.CostEstimate(flops=cost, bytes_accessed=3 * 2**20, transcendentals=2**20),
    )(*args)


def z_pairs(d):
    return [(x * ZS + z, x * ZS + (z + d) % ZS) for x in range(XS) for z in range(ZS)]


def x_pairs(d):
    return [(x * ZS + z, (x + d) % XS * ZS + z) for x in range(XS) for z in range(ZS)]


def z_send(a, d):
    return lax.ppermute(a, "ctx", z_pairs(d))


def x_send(a, d):
    return lax.ppermute(a, "ctx", x_pairs(d))


def head_send(a, d):
    pairs = [(i, i ^ 1 if d == 1 else (i + d) % 8) for i in range(8)]
    return lax.ppermute(a, "head", pairs)


def per_device(
    ssm_input,
    gate_input,
    in_state,
    out_state,
    step_size,
    log_decay,
    skip_gain,
    norm_gain,
    queries,
    keys,
    values,
):
    place = lax.axis_index("ctx")
    x, z = place // ZS, place % ZS

    def visible(d, low=0, high=XS):
        other = (z + d) % ZS
        return jnp.clip(x + (other < z), low, high) - low

    whole = [jnp.stack([visible(-i), visible(i)]).astype(jnp.int32) for i in (1, 2, 3)]
    tail = jnp.stack([visible(4, 0, 2), visible(4, 2, 4)]).astype(jnp.int32)
    here = x.astype(jnp.int32).reshape(1)
    struct = jax.ShapeDtypeStruct

    own = jnp.concatenate([keys, values], axis=0)
    around = x_send(own, 1), x_send(own, 2), x_send(own, -1)
    stacked, *sums = attend_first(queries, own)
    step, decay = step_size.T, log_decay.T
    msg = call(
        contrib_kernel,
        struct((CTX, 48, 128), BF16),
        100_000_000,
        ssm_input,
        in_state,
        step,
        decay,
        sums[2],
        limit=57,
    )
    column = call(
        column_kernel, struct((XS, 2 * BLOCK, DH), BF16), 1_000_000, here, own, *around, sums[1]
    )
    right1, left1 = z_send(column, 1), z_send(column, -1)
    msg = lax.all_to_all(msg, "ctx", 0, 0)
    right2, left2 = z_send(right1, 1), z_send(left1, -1)
    counts = jnp.concatenate([here, whole[0]])
    sums = attend_next(counts, stacked, (column, right1, left1), sums)
    state = call(scan_kernel, struct((CTX, 32, 128), BF16), 1_000_000, msg, sums[2])
    state = lax.all_to_all(state, "ctx", 0, 0)
    right3, left3 = z_send(right2, 1), z_send(left2, -1)
    sums = attend_next(whole[1], stacked, (right2, left2), sums)
    gated, squares = call(
        mix_kernel,
        [struct((BLOCK, WIDTH), BF16), struct((8, BLOCK), F32)],
        500_000_000,
        ssm_input,
        in_state,
        out_state,
        step,
        decay,
        gate_input,
        skip_gain.reshape(HEADS, 1),
        state.reshape(8, 128, 128),
        sums[2],
        limit=57,
    )
    squares = squares + head_send(squares, 1)
    squares = squares, *(head_send(squares, d) for d in (2, 4, 6))
    half = struct((XS // 2, 2 * BLOCK, DH), BF16)
    right4, left4 = call(halve_kernel, [half, half], 1_000_000, right3, left3)
    right4, left4 = z_send(right4, 1), z_send(left4, -1)
    sums = attend_next(whole[2], stacked, (right3, left3), sums)
    mamba_out = call(
        norm_kernel,
        struct((BLOCK, WIDTH), BF16),
        10_000_000,
        gated,
        *squares,
        norm_gain.reshape(1, WIDTH),
        limit=57,
    )
    counts = jnp.concatenate([here, *whole, tail])
    kvs = [column, right1, left1, right2, left2, right3, left3]
    attention_out = attend_last(counts, stacked, right4, left4, sums, own, kvs)
    return mamba_out, attention_out


def solution(mesh):
    both = P("ctx", "head")
    return jax.shard_map(
        per_device,
        mesh=mesh,
        in_specs=(both,) * 6 + (P("head"), P("head")) + (both,) * 3,
        out_specs=(both, both),
        check_vma=False,
    )
```

```python
import functools
import math

import jax
import jax.numpy as jnp
from jax import lax
from jax.experimental import pallas as pl
from jax.experimental.pallas import tpu as pltpu
from jax.sharding import PartitionSpec as P

MIXER_HEADS = 128
P_SIZE = 64
DH = 128
BLOCK = 256
XS = 4
ZS = 8
CTX = XS * ZS
HEADS = 16
WIDTH = HEADS * P_SIZE
LOG2E = math.log2(math.e)
SCALE = LOG2E * DH ** (-0.5)
F32 = jnp.float32
BF16 = jnp.bfloat16
HIGH = lax.Precision.HIGHEST
NT = (((1,), (1,)), ((), ()))
TN = (((0,), (0,)), ((), ()))


def dot(a, b, dims=(((1,), (0,)), ((), ())), precision=None):
    return lax.dot_general(a, b, dims, precision=precision, preferred_element_type=F32)


def halves(v):
    high = v.astype(BF16)
    return high, (v - high.astype(F32)).astype(BF16)


def expansion():
    lane = lax.broadcasted_iota(jnp.int32, (HEADS, WIDTH), 1)
    head = lax.broadcasted_iota(jnp.int32, (HEADS, WIDTH), 0)
    return jnp.where((lane >> 6) == head, 1.0, 0.0).astype(BF16)


def spread_heads(v):
    high, low = halves(v)
    return dot(high, expansion(), TN) + dot(low, expansion(), TN)


def running(a):
    row = lax.broadcasted_iota(jnp.int32, (BLOCK, BLOCK), 0)
    col = lax.broadcasted_iota(jnp.int32, (BLOCK, BLOCK), 1)
    cum = dot(jnp.where(col <= row, 1.0, 0.0), a, NT, precision=HIGH)
    cum_rows = dot(a, jnp.where(row <= col, 1.0, 0.0), precision=HIGH)
    return cum, cum_rows


def contrib_kernel(x_ref, b_ref, dt_ref, a_ref, tok_ref, msg_ref):
    _, cum = running(a_ref[...])
    last = cum[:, BLOCK - 1 :]
    xr = x_ref[...].astype(F32) * spread_heads(dt_ref[...] * jnp.exp(cum - last))
    fade_high, fade_low = halves(spread_heads(jnp.broadcast_to(jnp.exp(-last), (HEADS, 8))))
    contrib = dot(b_ref[...], xr.astype(BF16), TN).astype(BF16)
    for q in range(HEADS // 2):
        lanes = slice(q * 128, (q + 1) * 128)
        tail = jnp.concatenate([fade_high[:, lanes], fade_low[:, lanes]], axis=0)
        for r in range(4):
            msg_ref[q * 4 + r, 0:32, :] = contrib[r * 32 : (r + 1) * 32, lanes]
            msg_ref[q * 4 + r, 32:48, :] = tail


def scan_kernel(msg_ref, tok_ref, out_ref):
    state = jnp.zeros((32, 128), F32)
    for i in range(CTX):
        out_ref[i] = state.astype(BF16)
        piece = msg_ref[i].astype(F32)
        fade = piece[32:33] + piece[40:41]
        state = fade * state + piece[:32]


def mix_kernel(
    x_ref, b_ref, c_ref, dt_ref, a_ref, z_ref, skip_ref, st_ref, tok_ref, g_ref, ss_ref
):
    row = lax.broadcasted_iota(jnp.int32, (BLOCK, BLOCK), 0)
    col = lax.broadcasted_iota(jnp.int32, (BLOCK, BLOCK), 1)
    cum, cum_rows = running(a_ref[...])
    x = x_ref[...].astype(F32)
    xs = (x * spread_heads(dt_ref[...])).astype(BF16)
    ec = spread_heads(jnp.exp(-cum_rows))
    skip_high, skip_low = halves(jnp.broadcast_to(skip_ref[...], (8, HEADS)))
    skip = (dot(skip_high, expansion()) + dot(skip_low, expansion()))[:1]
    c = c_ref[...]
    affinity = jnp.where(col <= row, dot(c, b_ref[...], NT), 0.0)
    cum2 = cum * LOG2E
    cum2_rows = cum_rows * LOG2E
    half = BLOCK // 2
    low_lane = lax.broadcasted_iota(jnp.int32, (BLOCK, 128), 1) < P_SIZE
    squares = jnp.zeros((BLOCK, 128), F32)
    for q in range(HEADS // 2):
        lanes = slice(q * 128, (q + 1) * 128)
        xp = xs[:, lanes]
        parts = []
        for h in (2 * q, 2 * q + 1):
            across = cum2_rows[h : h + 1, :]
            down = cum2[:, h : h + 1]
            top = jnp.exp2(jnp.minimum(across[:, :half] - down[:half], 0.0)) * affinity[:half, :half]
            low = jnp.exp2(jnp.minimum(across - down[half:], 0.0)) * affinity[half:, :]
            parts.append(
                jnp.concatenate([dot(top.astype(BF16), xp[:half]), dot(low.astype(BF16), xp)], axis=0)
            )
        mixed = jnp.where(low_lane, parts[0], parts[1]) + skip[:, lanes] * x[:, lanes]
        mixed = mixed + dot(c, st_ref[q]) * ec[:, lanes]
        z = z_ref[:, lanes].astype(F32)
        gated = mixed * (z / (1.0 + jnp.exp(-z)))
        g_ref[:, lanes] = gated.astype(BF16)
        squares = squares + gated * gated
    high, low = halves(squares)
    ones = jnp.ones((8, 128), BF16)
    ss_ref[...] = dot(ones, high, NT) + dot(ones, low, NT)


def norm_kernel(g_ref, ss_ref, gain_ref, out_ref):
    total = dot(ss_ref[...], jnp.ones((8, 128), F32), TN, precision=HIGH)
    scale = lax.rsqrt(total * (1.0 / (MIXER_HEADS * P_SIZE)) + 1e-05)
    for q in range(HEADS // 2):
        lanes = slice(q * 128, (q + 1) * 128)
        out_ref[:, lanes] = (g_ref[:, lanes].astype(F32) * scale * gain_ref[:, lanes]).astype(BF16)


ROWS = 8 * BLOCK
LIMIT = 2.0**100


def keys_of(kv_ref, first, count):
    return kv_ref[pl.ds(first, count), :BLOCK, :].reshape(count * BLOCK, DH)


def values_of(kv_ref, first, count):
    return kv_ref[pl.ds(first, count), BLOCK:, :].reshape(count * BLOCK, DH)


def add_keys(qs_ref, k, v, l_ref, acc_ref, seen=None):
    lane = lax.broadcasted_iota(jnp.int32, k.shape, 1)
    ones = jnp.where(lane < 3, 1.0, 0.0).astype(BF16)
    score = dot(qs_ref[...], jnp.concatenate([k, ones], axis=1), NT)
    weights = []
    for j in range(0, k.shape[0], 128):
        weight = jnp.exp2(score[:, j : j + 128] * SCALE)
        if seen is not None:
            weight = jnp.where(seen[:, j : j + 128], weight, 0.0)
        weights.append(weight)
    l_ref[...] += sum(weights[1:], weights[0])
    acc_ref[...] += dot(jnp.concatenate([w.astype(BF16) for w in weights], axis=1), v)


def add_blocks(qs_ref, kv_ref, count, l_ref, acc_ref):
    @pl.loop(0, count // 2)
    def _(i):
        add_keys(qs_ref, keys_of(kv_ref, 2 * i, 2), values_of(kv_ref, 2 * i, 2), l_ref, acc_ref)

    @pl.when(count % 2 == 1)
    def _():
        at = count - 1
        add_keys(qs_ref, keys_of(kv_ref, at, 1), values_of(kv_ref, at, 1), l_ref, acc_ref)


def careful(qs_ref, kv_ref, count, m_ref, l_ref, acc_ref, diagonal=None):
    @pl.loop(0, 8)
    def _(h):
        rows = pl.ds(pl.multiple_of(h * BLOCK, BLOCK), BLOCK)

        def one(k, v, seen):
            score = dot(qs_ref[rows, :DH], k, NT) * SCALE
            if seen is not None:
                score = jnp.where(seen, score, -1e30)
            m_old = m_ref[rows, :]
            m_new = jnp.maximum(m_old, jnp.max(score, axis=1, keepdims=True))
            weight = jnp.exp2(score - m_new[:, :1])
            shrink = jnp.exp2(m_old - m_new)
            l_ref[rows, :] = l_ref[rows, :] * shrink + (weight[:, :128] + weight[:, 128:])
            acc_ref[rows, :] = acc_ref[rows, :] * shrink + dot(weight.astype(BF16), v)
            m_ref[rows, :] = m_new

        if diagonal is not None:
            one(*diagonal)

        @pl.loop(0, count)
        def _(b):
            one(keys_of(kv_ref, b, 1), values_of(kv_ref, b, 1), None)


def first_kernel(q_ref, own_ref, qs_ref, l_ref, acc_ref, tok_ref):
    tok_ref[...] = jnp.zeros((8, 128), F32)
    k = own_ref[:BLOCK, :]
    key = k.astype(F32)
    lane = lax.broadcasted_iota(jnp.int32, (BLOCK, DH), 1)
    for h in range(8):
        rows = slice(h * BLOCK, (h + 1) * BLOCK)
        q = q_ref[:, h * DH : (h + 1) * DH]
        qs_ref[rows, :DH] = q
        rest = -jnp.broadcast_to(jnp.sum(q.astype(F32) * key, axis=1, keepdims=True), (BLOCK, DH))
        pieces = jnp.zeros((BLOCK, DH), F32)
        for i in range(3):
            piece = rest.astype(BF16).astype(F32)
            pieces = jnp.where(lane == i, piece, pieces)
            rest = rest - piece
        qs_ref[rows, DH:] = pieces.astype(BF16)
    l_ref[...] = jnp.zeros((ROWS, DH), F32)
    acc_ref[...] = jnp.zeros((ROWS, DH), F32)
    row = lax.broadcasted_iota(jnp.int32, (ROWS, BLOCK), 0) & (BLOCK - 1)
    col = lax.broadcasted_iota(jnp.int32, (ROWS, BLOCK), 1)
    add_keys(qs_ref, k, own_ref[BLOCK:, :], l_ref, acc_ref, col <= row)


def next_kernel(n, counts_ref, qs_ref, *refs):
    kv_refs, (_, _, tok_in, l_ref, acc_ref, tok_ref) = refs[:n], refs[n:]
    tok_ref[...] = tok_in[...]
    for i, kv_ref in enumerate(kv_refs):
        add_blocks(qs_ref, kv_ref, counts_ref[i], l_ref, acc_ref)


def last_kernel(
    n, counts_ref, qs_ref, right_ref, left_ref, l_in, acc_in, tok_in, own_ref, *refs
):
    kv_refs, (out_ref, l_ref, acc_ref, m_ref, kv_ref, sem) = refs[:n], refs[n:]
    add_blocks(qs_ref, right_ref, counts_ref[n], l_ref, acc_ref)
    add_blocks(qs_ref, left_ref, counts_ref[n + 1], l_ref, acc_ref)

    @pl.when(jnp.logical_not(jnp.max(l_ref[...]) <= LIMIT))
    def _():
        l_ref[...] = jnp.zeros((ROWS, DH), F32)
        acc_ref[...] = jnp.zeros((ROWS, DH), F32)
        m_ref[...] = jnp.full((ROWS, DH), -1e30, F32)
        row = lax.broadcasted_iota(jnp.int32, (BLOCK, BLOCK), 0)
        col = lax.broadcasted_iota(jnp.int32, (BLOCK, BLOCK), 1)
        own = (own_ref[:BLOCK, :], own_ref[BLOCK:, :], col <= row)
        for i in range(n):
            copy = pltpu.make_async_copy(kv_refs[i], kv_ref, sem)
            copy.start()
            copy.wait()
            diagonal = own if i == 0 else None
            careful(qs_ref, kv_ref, counts_ref[i], m_ref, l_ref, acc_ref, diagonal)
        careful(qs_ref, right_ref, counts_ref[n], m_ref, l_ref, acc_ref)
        careful(qs_ref, left_ref, counts_ref[n + 1], m_ref, l_ref, acc_ref)

    for h in range(8):
        rows = slice(h * BLOCK, (h + 1) * BLOCK)
        total = jnp.sum(l_ref[rows, :], axis=1, keepdims=True)
        out_ref[:, h * DH : (h + 1) * DH] = (acc_ref[rows, :] / total).astype(BF16)


SUMS = pltpu.VMEM((ROWS, DH), F32)
TOKEN = jax.ShapeDtypeStruct((8, 128), F32)
SMEM = pl.BlockSpec(memory_space=pltpu.SMEM)
VMEM = pl.BlockSpec(memory_space=pltpu.VMEM)
PLAIN = pl.BlockSpec()
ANY = pl.BlockSpec(memory_space=pl.ANY)
KERNEL = pltpu.CompilerParams(vmem_limit_bytes=28 * 2**20)


def cost_of(blocks):
    work = blocks * ROWS * BLOCK
    return pl.CostEstimate(flops=4 * work * DH, bytes_accessed=2**20, transcendentals=work)


def attend_first(queries, own):
    return pl.pallas_call(
        first_kernel,
        in_specs=[PLAIN, PLAIN],
        out_specs=[VMEM] * 3 + [PLAIN],
        out_shape=[pltpu.VMEM((ROWS, 2 * DH), BF16), SUMS, SUMS, TOKEN],
        compiler_params=KERNEL,
        cost_estimate=cost_of(1),
        name="attend_first",
    )(queries, own)


def attend_next(counts, stacked, kvs, sums):
    n = len(kvs)
    return pl.pallas_call(
        functools.partial(next_kernel, n),
        in_specs=[SMEM, VMEM] + [PLAIN] * n + [VMEM] * 2 + [PLAIN],
        out_specs=[VMEM] * 2 + [PLAIN],
        out_shape=[SUMS, SUMS, TOKEN],
        input_output_aliases={n + 2: 0, n + 3: 1},
        compiler_params=KERNEL,
        cost_estimate=cost_of(sum(kv.shape[0] for kv in kvs)),
        name="attend_next",
    )(counts, stacked, *kvs, *sums)


def attend_last(counts, stacked, right, left, sums, own, kvs):
    return pl.pallas_call(
        functools.partial(last_kernel, len(kvs)),
        in_specs=[SMEM, VMEM, PLAIN, PLAIN, VMEM, VMEM, PLAIN, PLAIN] + [ANY] * len(kvs),
        out_specs=[PLAIN, VMEM, VMEM],
        out_shape=[jax.ShapeDtypeStruct((BLOCK, 8 * DH), BF16), SUMS, SUMS],
        scratch_shapes=[
            pltpu.VMEM((ROWS, DH), F32),
            pltpu.VMEM((XS, 2 * BLOCK, DH), BF16),
            pltpu.SemaphoreType.DMA,
        ],
        input_output_aliases={4: 1, 5: 2},
        compiler_params=KERNEL,
        cost_estimate=cost_of(4),
        name="attend_last",
    )(counts, stacked, right, left, *sums, own, *kvs)[0]


def column_kernel(x_ref, own_ref, one_ref, two_ref, three_ref, tok_ref, out_ref):
    x = x_ref[0]
    for d, ref in enumerate((own_ref, one_ref, two_ref, three_ref)):
        out_ref[lax.rem(x + XS - d, XS)] = ref[...]


def halve_kernel(right_ref, left_ref, low_ref, high_ref):
    low_ref[...] = right_ref[: XS // 2]
    high_ref[...] = left_ref[XS // 2 :]


def call(kernel, outs, cost, *args, limit=28):
    return pl.pallas_call(
        kernel,
        in_specs=[SMEM if arg.dtype == jnp.int32 else PLAIN for arg in args],
        out_shape=outs,
        compiler_params=pltpu.CompilerParams(vmem_limit_bytes=limit * 2**20),
        cost_estimate=pl.CostEstimate(flops=cost, bytes_accessed=3 * 2**20, transcendentals=2**20),
    )(*args)


def z_pairs(d):
    return [(x * ZS + z, x * ZS + (z + d) % ZS) for x in range(XS) for z in range(ZS)]


def x_pairs(d):
    return [(x * ZS + z, (x + d) % XS * ZS + z) for x in range(XS) for z in range(ZS)]


def z_send(a, d):
    return lax.ppermute(a, "ctx", z_pairs(d))


def x_send(a, d):
    return lax.ppermute(a, "ctx", x_pairs(d))


def per_device(
    ssm_input,
    gate_input,
    in_state,
    out_state,
    step_size,
    log_decay,
    skip_gain,
    norm_gain,
    queries,
    keys,
    values,
):
    place = lax.axis_index("ctx")
    x, z = place // ZS, place % ZS

    def visible(d, low=0, high=XS):
        other = (z + d) % ZS
        return jnp.clip(x + (other < z), low, high) - low

    whole = [jnp.stack([visible(-i), visible(i)]).astype(jnp.int32) for i in (1, 2, 3)]
    tail = jnp.stack([visible(4, 0, 2), visible(4, 2, 4)]).astype(jnp.int32)
    here = x.astype(jnp.int32).reshape(1)
    struct = jax.ShapeDtypeStruct

    own = jnp.concatenate([keys, values], axis=0)
    around = x_send(own, 1), x_send(own, 2), x_send(own, -1)
    stacked, *sums = attend_first(queries, own)
    step, decay = step_size.T, log_decay.T
    msg = call(
        contrib_kernel,
        struct((CTX, 48, 128), BF16),
        100_000_000,
        ssm_input,
        in_state,
        step,
        decay,
        sums[2],
        limit=46,
    )
    column = call(
        column_kernel, struct((XS, 2 * BLOCK, DH), BF16), 1_000_000, here, own, *around, sums[1]
    )
    right1, left1 = z_send(column, 1), z_send(column, -1)
    msg = lax.all_to_all(msg, "ctx", 0, 0)
    right2, left2 = z_send(right1, 1), z_send(left1, -1)
    counts = jnp.concatenate([here, whole[0]])
    sums = attend_next(counts, stacked, (column, right1, left1), sums)
    state = call(scan_kernel, struct((CTX, 32, 128), BF16), 1_000_000, msg, sums[2])
    state = lax.all_to_all(state, "ctx", 0, 0)
    right3, left3 = z_send(right2, 1), z_send(left2, -1)
    sums = attend_next(whole[1], stacked, (right2, left2), sums)
    gated, squares = call(
        mix_kernel,
        [struct((BLOCK, WIDTH), BF16), struct((8, BLOCK), F32)],
        500_000_000,
        ssm_input,
        in_state,
        out_state,
        step,
        decay,
        gate_input,
        skip_gain.reshape(1, HEADS),
        state.reshape(8, 128, 128),
        sums[2],
        limit=46,
    )
    squares = lax.all_gather(squares[0], "head")
    half = struct((XS // 2, 2 * BLOCK, DH), BF16)
    right4, left4 = call(halve_kernel, [half, half], 1_000_000, right3, left3)
    right4, left4 = z_send(right4, 1), z_send(left4, -1)
    sums = attend_next(whole[2], stacked, (right3, left3), sums)
    mamba_out = call(
        norm_kernel,
        struct((BLOCK, WIDTH), BF16),
        10_000_000,
        gated,
        squares,
        norm_gain.reshape(1, WIDTH),
        limit=46,
    )
    counts = jnp.concatenate([here, *whole, tail])
    kvs = [column, right1, left1, right2, left2, right3, left3]
    attention_out = attend_last(counts, stacked, right4, left4, sums, own, kvs)
    return mamba_out, attention_out


def solution(mesh):
    both = P("ctx", "head")
    return jax.shard_map(
        per_device,
        mesh=mesh,
        in_specs=(both,) * 6 + (P("head"), P("head")) + (both,) * 3,
        out_specs=(both, both),
        check_vma=False,
    )
```

```python
import functools
import math

import jax
import jax.numpy as jnp
from jax import lax
from jax.experimental import pallas as pl
from jax.experimental.pallas import tpu as pltpu
from jax.sharding import PartitionSpec as P

MIXER_HEADS = 128
P_SIZE = 64
DH = 128
BLOCK = 256
XS = 4
ZS = 8
CTX = XS * ZS
HEADS = 16
WIDTH = HEADS * P_SIZE
LOG2E = math.log2(math.e)
SCALE = LOG2E * DH ** (-0.5)
F32 = jnp.float32
BF16 = jnp.bfloat16
HIGH = lax.Precision.HIGHEST
NT = (((1,), (1,)), ((), ()))
TN = (((0,), (0,)), ((), ()))


def dot(a, b, dims=(((1,), (0,)), ((), ())), precision=None):
    return lax.dot_general(a, b, dims, precision=precision, preferred_element_type=F32)


def halves(v):
    high = v.astype(BF16)
    return high, (v - high.astype(F32)).astype(BF16)


def expansion():
    lane = lax.broadcasted_iota(jnp.int32, (HEADS, WIDTH), 1)
    head = lax.broadcasted_iota(jnp.int32, (HEADS, WIDTH), 0)
    return jnp.where((lane >> 6) == head, 1.0, 0.0).astype(BF16)


def spread_heads(v):
    high, low = halves(v)
    return dot(high, expansion(), TN) + dot(low, expansion(), TN)


def running(a):
    row = lax.broadcasted_iota(jnp.int32, (BLOCK, BLOCK), 0)
    col = lax.broadcasted_iota(jnp.int32, (BLOCK, BLOCK), 1)
    cum = dot(jnp.where(col <= row, 1.0, 0.0), a, NT, precision=HIGH)
    cum_rows = dot(a, jnp.where(row <= col, 1.0, 0.0), precision=HIGH)
    return cum, cum_rows


def contrib_kernel(x_ref, b_ref, dt_ref, a_ref, tok_ref, msg_ref):
    _, cum = running(a_ref[...])
    last = cum[:, BLOCK - 1 :]
    xr = x_ref[...].astype(F32) * spread_heads(dt_ref[...] * jnp.exp(cum - last))
    fade_high, fade_low = halves(spread_heads(jnp.broadcast_to(jnp.exp(-last), (HEADS, 8))))
    contrib = dot(b_ref[...], xr.astype(BF16), TN).astype(BF16)
    for q in range(HEADS // 2):
        lanes = slice(q * 128, (q + 1) * 128)
        tail = jnp.concatenate([fade_high[:, lanes], fade_low[:, lanes]], axis=0)
        for r in range(4):
            msg_ref[q * 4 + r, 0:32, :] = contrib[r * 32 : (r + 1) * 32, lanes]
            msg_ref[q * 4 + r, 32:48, :] = tail


def scan_kernel(msg_ref, tok_ref, out_ref):
    state = jnp.zeros((32, 128), F32)
    for i in range(CTX):
        out_ref[i] = state.astype(BF16)
        piece = msg_ref[i].astype(F32)
        fade = piece[32:33] + piece[40:41]
        state = fade * state + piece[:32]


def mix_kernel(
    x_ref, b_ref, c_ref, dt_ref, a_ref, z_ref, skip_ref, st_ref, tok_ref, g_ref, ss_ref
):
    row = lax.broadcasted_iota(jnp.int32, (BLOCK, BLOCK), 0)
    col = lax.broadcasted_iota(jnp.int32, (BLOCK, BLOCK), 1)
    cum, cum_rows = running(a_ref[...])
    x = x_ref[...].astype(F32)
    xs = (x * spread_heads(dt_ref[...])).astype(BF16)
    ec = spread_heads(jnp.exp(-cum_rows))
    skip_high, skip_low = halves(jnp.broadcast_to(skip_ref[...], (8, HEADS)))
    skip = (dot(skip_high, expansion()) + dot(skip_low, expansion()))[:1]
    c = c_ref[...]
    affinity = jnp.where(col <= row, dot(c, b_ref[...], NT), 0.0)
    cum2 = cum * LOG2E
    cum2_rows = cum_rows * LOG2E
    half = BLOCK // 2
    low_lane = lax.broadcasted_iota(jnp.int32, (BLOCK, 128), 1) < P_SIZE
    squares = jnp.zeros((BLOCK, 128), F32)
    for q in range(HEADS // 2):
        lanes = slice(q * 128, (q + 1) * 128)
        xp = xs[:, lanes]
        parts = []
        for h in (2 * q, 2 * q + 1):
            across = cum2_rows[h : h + 1, :]
            down = cum2[:, h : h + 1]
            top = jnp.exp2(jnp.minimum(across[:, :half] - down[:half], 0.0)) * affinity[:half, :half]
            low = jnp.exp2(jnp.minimum(across - down[half:], 0.0)) * affinity[half:, :]
            parts.append(
                jnp.concatenate([dot(top.astype(BF16), xp[:half]), dot(low.astype(BF16), xp)], axis=0)
            )
        mixed = jnp.where(low_lane, parts[0], parts[1]) + skip[:, lanes] * x[:, lanes]
        mixed = mixed + dot(c, st_ref[q]) * ec[:, lanes]
        z = z_ref[:, lanes].astype(F32)
        gated = mixed * (z / (1.0 + jnp.exp(-z)))
        g_ref[:, lanes] = gated.astype(BF16)
        squares = squares + gated * gated
    high, low = halves(squares)
    ones = jnp.ones((8, 128), BF16)
    ss_ref[...] = dot(ones, high, NT) + dot(ones, low, NT)


def norm_kernel(g_ref, ss_ref, gain_ref, out_ref):
    total = dot(ss_ref[...], jnp.ones((8, 128), F32), TN, precision=HIGH)
    scale = lax.rsqrt(total * (1.0 / (MIXER_HEADS * P_SIZE)) + 1e-05)
    for q in range(HEADS // 2):
        lanes = slice(q * 128, (q + 1) * 128)
        out_ref[:, lanes] = (g_ref[:, lanes].astype(F32) * scale * gain_ref[:, lanes]).astype(BF16)


ROWS = 8 * BLOCK
LIMIT = 2.0**100


def keys_of(kv_ref, first, count):
    return kv_ref[pl.ds(first, count), :BLOCK, :].reshape(count * BLOCK, DH)


def values_of(kv_ref, first, count):
    return kv_ref[pl.ds(first, count), BLOCK:, :].reshape(count * BLOCK, DH)


def add_keys(qs_ref, k, v, l_ref, acc_ref, seen=None):
    lane = lax.broadcasted_iota(jnp.int32, k.shape, 1)
    ones = jnp.where(lane < 3, 1.0, 0.0).astype(BF16)
    score = dot(qs_ref[...], jnp.concatenate([k, ones], axis=1), NT)
    weights = []
    for j in range(0, k.shape[0], 128):
        weight = jnp.exp2(score[:, j : j + 128] * SCALE)
        if seen is not None:
            weight = jnp.where(seen[:, j : j + 128], weight, 0.0)
        weights.append(weight)
    l_ref[...] += sum(weights[1:], weights[0])
    acc_ref[...] += dot(jnp.concatenate([w.astype(BF16) for w in weights], axis=1), v)


def add_blocks(qs_ref, kv_ref, count, l_ref, acc_ref):
    @pl.loop(0, count // 2)
    def _(i):
        add_keys(qs_ref, keys_of(kv_ref, 2 * i, 2), values_of(kv_ref, 2 * i, 2), l_ref, acc_ref)

    @pl.when(count % 2 == 1)
    def _():
        at = count - 1
        add_keys(qs_ref, keys_of(kv_ref, at, 1), values_of(kv_ref, at, 1), l_ref, acc_ref)


def careful(qs_ref, kv_ref, count, m_ref, l_ref, acc_ref, diagonal=None):
    @pl.loop(0, 8)
    def _(h):
        rows = pl.ds(pl.multiple_of(h * BLOCK, BLOCK), BLOCK)

        def one(k, v, seen):
            score = dot(qs_ref[rows, :DH], k, NT) * SCALE
            if seen is not None:
                score = jnp.where(seen, score, -1e30)
            m_old = m_ref[rows, :]
            m_new = jnp.maximum(m_old, jnp.max(score, axis=1, keepdims=True))
            weight = jnp.exp2(score - m_new[:, :1])
            shrink = jnp.exp2(m_old - m_new)
            l_ref[rows, :] = l_ref[rows, :] * shrink + (weight[:, :128] + weight[:, 128:])
            acc_ref[rows, :] = acc_ref[rows, :] * shrink + dot(weight.astype(BF16), v)
            m_ref[rows, :] = m_new

        if diagonal is not None:
            one(*diagonal)

        @pl.loop(0, count)
        def _(b):
            one(keys_of(kv_ref, b, 1), values_of(kv_ref, b, 1), None)


def first_kernel(q_ref, own_ref, qs_ref, l_ref, acc_ref, tok_ref):
    tok_ref[...] = jnp.zeros((8, 128), F32)
    k = own_ref[:BLOCK, :]
    key = k.astype(F32)
    lane = lax.broadcasted_iota(jnp.int32, (BLOCK, DH), 1)
    for h in range(8):
        rows = slice(h * BLOCK, (h + 1) * BLOCK)
        q = q_ref[:, h * DH : (h + 1) * DH]
        qs_ref[rows, :DH] = q
        rest = -jnp.broadcast_to(jnp.sum(q.astype(F32) * key, axis=1, keepdims=True), (BLOCK, DH))
        pieces = jnp.zeros((BLOCK, DH), F32)
        for i in range(3):
            piece = rest.astype(BF16).astype(F32)
            pieces = jnp.where(lane == i, piece, pieces)
            rest = rest - piece
        qs_ref[rows, DH:] = pieces.astype(BF16)
    l_ref[...] = jnp.zeros((ROWS, DH), F32)
    acc_ref[...] = jnp.zeros((ROWS, DH), F32)
    row = lax.broadcasted_iota(jnp.int32, (ROWS, BLOCK), 0) & (BLOCK - 1)
    col = lax.broadcasted_iota(jnp.int32, (ROWS, BLOCK), 1)
    add_keys(qs_ref, k, own_ref[BLOCK:, :], l_ref, acc_ref, col <= row)


def next_kernel(n, counts_ref, qs_ref, *refs):
    kv_refs, (_, _, l_ref, acc_ref, tok_ref) = refs[:n], refs[n:]
    tok_ref[...] = jnp.zeros((8, 128), F32)
    for i, kv_ref in enumerate(kv_refs):
        add_blocks(qs_ref, kv_ref, counts_ref[i], l_ref, acc_ref)


def last_kernel(
    n, counts_ref, qs_ref, right_ref, left_ref, l_in, acc_in, own_ref, *refs
):
    kv_refs, (out_ref, l_ref, acc_ref, m_ref, kv_ref, held_ref, sem) = refs[:n], refs[n:]
    add_blocks(qs_ref, right_ref, counts_ref[n], l_ref, acc_ref)
    add_blocks(qs_ref, left_ref, counts_ref[n + 1], l_ref, acc_ref)

    @pl.when(jnp.logical_not(jnp.max(l_ref[...]) <= LIMIT))
    def _():
        l_ref[...] = jnp.zeros((ROWS, DH), F32)
        acc_ref[...] = jnp.zeros((ROWS, DH), F32)
        m_ref[...] = jnp.full((ROWS, DH), -1e30, F32)
        row = lax.broadcasted_iota(jnp.int32, (BLOCK, BLOCK), 0)
        col = lax.broadcasted_iota(jnp.int32, (BLOCK, BLOCK), 1)
        copy = pltpu.make_async_copy(own_ref, held_ref, sem)
        copy.start()
        copy.wait()
        own = (held_ref[:BLOCK, :], held_ref[BLOCK:, :], col <= row)
        for i in range(n):
            copy = pltpu.make_async_copy(kv_refs[i], kv_ref, sem)
            copy.start()
            copy.wait()
            diagonal = own if i == 0 else None
            careful(qs_ref, kv_ref, counts_ref[i], m_ref, l_ref, acc_ref, diagonal)
        careful(qs_ref, right_ref, counts_ref[n], m_ref, l_ref, acc_ref)
        careful(qs_ref, left_ref, counts_ref[n + 1], m_ref, l_ref, acc_ref)

    for h in range(8):
        rows = slice(h * BLOCK, (h + 1) * BLOCK)
        total = jnp.sum(l_ref[rows, :], axis=1, keepdims=True)
        out_ref[:, h * DH : (h + 1) * DH] = (acc_ref[rows, :] / total).astype(BF16)


SUMS = pltpu.VMEM((ROWS, DH), F32)
TOKEN = jax.ShapeDtypeStruct((8, 128), F32)
SMEM = pl.BlockSpec(memory_space=pltpu.SMEM)
VMEM = pl.BlockSpec(memory_space=pltpu.VMEM)
PLAIN = pl.BlockSpec()
ANY = pl.BlockSpec(memory_space=pl.ANY)
KERNEL = pltpu.CompilerParams(vmem_limit_bytes=28 * 2**20)


def cost_of(blocks):
    work = blocks * ROWS * BLOCK
    return pl.CostEstimate(flops=4 * work * DH, bytes_accessed=2**20, transcendentals=work)


def attend_first(queries, own):
    return pl.pallas_call(
        first_kernel,
        in_specs=[PLAIN, PLAIN],
        out_specs=[VMEM] * 3 + [PLAIN],
        out_shape=[pltpu.VMEM((ROWS, 2 * DH), BF16), SUMS, SUMS, TOKEN],
        compiler_params=KERNEL,
        cost_estimate=cost_of(1),
        name="attend_first",
    )(queries, own)


def attend_next(counts, stacked, kvs, sums):
    n = len(kvs)
    return pl.pallas_call(
        functools.partial(next_kernel, n),
        in_specs=[SMEM, VMEM] + [PLAIN] * n + [VMEM] * 2,
        out_specs=[VMEM] * 2 + [PLAIN],
        out_shape=[SUMS, SUMS, TOKEN],
        input_output_aliases={n + 2: 0, n + 3: 1},
        compiler_params=KERNEL,
        cost_estimate=cost_of(sum(kv.shape[0] for kv in kvs)),
        name="attend_next",
    )(counts, stacked, *kvs, *sums[:2])


def attend_last(counts, stacked, right, left, sums, own, kvs):
    return pl.pallas_call(
        functools.partial(last_kernel, len(kvs)),
        in_specs=[SMEM, VMEM, PLAIN, PLAIN, VMEM, VMEM, ANY] + [ANY] * len(kvs),
        out_specs=[PLAIN, VMEM, VMEM],
        out_shape=[jax.ShapeDtypeStruct((BLOCK, 8 * DH), BF16), SUMS, SUMS],
        scratch_shapes=[
            pltpu.VMEM((ROWS, DH), F32),
            pltpu.VMEM((XS, 2 * BLOCK, DH), BF16),
            pltpu.VMEM((2 * BLOCK, DH), BF16),
            pltpu.SemaphoreType.DMA,
        ],
        input_output_aliases={4: 1, 5: 2},
        compiler_params=KERNEL,
        cost_estimate=cost_of(4),
        name="attend_last",
    )(counts, stacked, right, left, *sums[:2], own, *kvs)[0]


def column_kernel(x_ref, own_ref, one_ref, two_ref, three_ref, tok_ref, out_ref):
    x = x_ref[0]
    for d, ref in enumerate((own_ref, one_ref, two_ref, three_ref)):
        out_ref[lax.rem(x + XS - d, XS)] = ref[...]


def halve_kernel(right_ref, left_ref, low_ref, high_ref):
    low_ref[...] = right_ref[: XS // 2]
    high_ref[...] = left_ref[XS // 2 :]


def spec_of(arg):
    if arg.dtype == jnp.int32:
        return SMEM
    return ANY if arg.shape == TOKEN.shape else PLAIN


def call(kernel, outs, cost, *args, limit=28):
    return pl.pallas_call(
        kernel,
        in_specs=[spec_of(arg) for arg in args],
        out_shape=outs,
        compiler_params=pltpu.CompilerParams(vmem_limit_bytes=limit * 2**20),
        cost_estimate=pl.CostEstimate(flops=cost, bytes_accessed=3 * 2**20, transcendentals=2**20),
    )(*args)


def z_pairs(d):
    return [(x * ZS + z, x * ZS + (z + d) % ZS) for x in range(XS) for z in range(ZS)]


def x_pairs(d):
    return [(x * ZS + z, (x + d) % XS * ZS + z) for x in range(XS) for z in range(ZS)]


def z_send(a, d):
    return lax.ppermute(a, "ctx", z_pairs(d))


def x_send(a, d):
    return lax.ppermute(a, "ctx", x_pairs(d))


def per_device(
    ssm_input,
    gate_input,
    in_state,
    out_state,
    step_size,
    log_decay,
    skip_gain,
    norm_gain,
    queries,
    keys,
    values,
):
    place = lax.axis_index("ctx")
    x, z = place // ZS, place % ZS

    def visible(d, low=0, high=XS):
        other = (z + d) % ZS
        return jnp.clip(x + (other < z), low, high) - low

    whole = [jnp.stack([visible(-i), visible(i)]).astype(jnp.int32) for i in (1, 2, 3)]
    tail = jnp.stack([visible(4, 0, 2), visible(4, 2, 4)]).astype(jnp.int32)
    here = x.astype(jnp.int32).reshape(1)
    struct = jax.ShapeDtypeStruct

    own = jnp.concatenate([keys, values], axis=0)
    around = x_send(own, 1), x_send(own, 2), x_send(own, -1)
    stacked, *sums = attend_first(queries, own)
    step, decay = step_size.T, log_decay.T
    msg = call(
        contrib_kernel,
        struct((CTX, 48, 128), BF16),
        100_000_000,
        ssm_input,
        in_state,
        step,
        decay,
        sums[2],
        limit=46,
    )
    column = call(
        column_kernel, struct((XS, 2 * BLOCK, DH), BF16), 1_000_000, here, own, *around, sums[1]
    )
    right1, left1 = z_send(column, 1), z_send(column, -1)
    msg = lax.all_to_all(msg, "ctx", 0, 0)
    right2, left2 = z_send(right1, 1), z_send(left1, -1)
    counts = jnp.concatenate([here, whole[0]])
    sums = attend_next(counts, stacked, (column, right1, left1), sums)
    state = call(scan_kernel, struct((CTX, 32, 128), BF16), 1_000_000, msg, sums[2])
    state = lax.all_to_all(state, "ctx", 0, 0)
    right3, left3 = z_send(right2, 1), z_send(left2, -1)
    sums = attend_next(whole[1], stacked, (right2, left2), sums)
    gated, squares = call(
        mix_kernel,
        [struct((BLOCK, WIDTH), BF16), struct((8, BLOCK), F32)],
        500_000_000,
        ssm_input,
        in_state,
        out_state,
        step,
        decay,
        gate_input,
        skip_gain.reshape(1, HEADS),
        state.reshape(8, 128, 128),
        sums[2],
        limit=62,
    )
    squares = lax.all_gather(squares[0], "head")
    half = struct((XS // 2, 2 * BLOCK, DH), BF16)
    right4, left4 = call(halve_kernel, [half, half], 1_000_000, right3, left3)
    right4, left4 = z_send(right4, 1), z_send(left4, -1)
    sums = attend_next(whole[2], stacked, (right3, left3), sums)
    mamba_out = call(
        norm_kernel,
        struct((BLOCK, WIDTH), BF16),
        10_000_000,
        gated,
        squares,
        norm_gain.reshape(1, WIDTH),
        limit=46,
    )
    counts = jnp.concatenate([here, *whole, tail])
    kvs = [column, right1, left1, right2, left2, right3, left3]
    attention_out = attend_last(counts, stacked, right4, left4, sums, own, kvs)
    return mamba_out, attention_out


def solution(mesh):
    both = P("ctx", "head")
    return jax.shard_map(
        per_device,
        mesh=mesh,
        in_specs=(both,) * 6 + (P("head"), P("head")) + (both,) * 3,
        out_specs=(both, both),
        check_vma=False,
    )
```

```python
import functools
import math

import jax
import jax.numpy as jnp
from jax import lax
from jax.experimental import pallas as pl
from jax.experimental.pallas import tpu as pltpu
from jax.sharding import PartitionSpec as P

MIXER_HEADS = 128
P_SIZE = 64
DH = 128
BLOCK = 256
XS = 4
ZS = 8
CTX = XS * ZS
HEADS = 16
WIDTH = HEADS * P_SIZE
LOG2E = math.log2(math.e)
SCALE = LOG2E * DH ** (-0.5)
F32 = jnp.float32
BF16 = jnp.bfloat16
HIGH = lax.Precision.HIGHEST
NT = (((1,), (1,)), ((), ()))
TN = (((0,), (0,)), ((), ()))


def dot(a, b, dims=(((1,), (0,)), ((), ())), precision=None):
    return lax.dot_general(a, b, dims, precision=precision, preferred_element_type=F32)


def halves(v):
    high = v.astype(BF16)
    return high, (v - high.astype(F32)).astype(BF16)


def expansion():
    lane = lax.broadcasted_iota(jnp.int32, (HEADS, WIDTH), 1)
    head = lax.broadcasted_iota(jnp.int32, (HEADS, WIDTH), 0)
    return jnp.where((lane >> 6) == head, 1.0, 0.0).astype(BF16)


def spread_heads(v):
    high, low = halves(v)
    return dot(high, expansion(), TN) + dot(low, expansion(), TN)


def running(a):
    row = lax.broadcasted_iota(jnp.int32, (BLOCK, BLOCK), 0)
    col = lax.broadcasted_iota(jnp.int32, (BLOCK, BLOCK), 1)
    cum = dot(jnp.where(col <= row, 1.0, 0.0), a, NT, precision=HIGH)
    cum_rows = dot(a, jnp.where(row <= col, 1.0, 0.0), precision=HIGH)
    return cum, cum_rows


def contrib_kernel(x_ref, b_ref, dt_ref, a_ref, tok_ref, msg_ref):
    _, cum = running(a_ref[...])
    last = cum[:, BLOCK - 1 :]
    xr = x_ref[...].astype(F32) * spread_heads(dt_ref[...] * jnp.exp(cum - last))
    fade_high, fade_low = halves(spread_heads(jnp.broadcast_to(jnp.exp(-last), (HEADS, 8))))
    contrib = dot(b_ref[...], xr.astype(BF16), TN).astype(BF16)
    for q in range(HEADS // 2):
        lanes = slice(q * 128, (q + 1) * 128)
        tail = jnp.concatenate([fade_high[:, lanes], fade_low[:, lanes]], axis=0)
        for r in range(4):
            msg_ref[q * 4 + r, 0:32, :] = contrib[r * 32 : (r + 1) * 32, lanes]
            msg_ref[q * 4 + r, 32:48, :] = tail


def scan_kernel(msg_ref, tok_ref, out_ref):
    state = jnp.zeros((32, 128), F32)
    for i in range(CTX):
        out_ref[i] = state.astype(BF16)
        piece = msg_ref[i].astype(F32)
        fade = piece[32:33] + piece[40:41]
        state = fade * state + piece[:32]


def mix_kernel(
    x_in, b_ref, c_ref, dt_ref, a_ref, z_in, skip_ref, st_in, tok_ref, g_ref, ss_ref, *held
):
    x_ref, z_ref, st_ref, sems = held
    pairs = ((x_in, x_ref), (st_in, st_ref), (z_in, z_ref))
    copies = [pltpu.make_async_copy(p, q, sems.at[i]) for i, (p, q) in enumerate(pairs)]
    for copy in copies:
        copy.start()
    row = lax.broadcasted_iota(jnp.int32, (BLOCK, BLOCK), 0)
    col = lax.broadcasted_iota(jnp.int32, (BLOCK, BLOCK), 1)
    cum, cum_rows = running(a_ref[...])
    ec = spread_heads(jnp.exp(-cum_rows))
    skip_high, skip_low = halves(jnp.broadcast_to(skip_ref[...], (8, HEADS)))
    skip = (dot(skip_high, expansion()) + dot(skip_low, expansion()))[:1]
    c = c_ref[...]
    affinity = jnp.where(col <= row, dot(c, b_ref[...], NT), 0.0)
    step = spread_heads(dt_ref[...])
    copies[0].wait()
    x = x_ref[...].astype(F32)
    xs = (x * step).astype(BF16)
    copies[1].wait()
    copies[2].wait()
    cum2 = cum * LOG2E
    cum2_rows = cum_rows * LOG2E
    half = BLOCK // 2
    low_lane = lax.broadcasted_iota(jnp.int32, (BLOCK, 128), 1) < P_SIZE
    squares = jnp.zeros((BLOCK, 128), F32)
    for q in range(HEADS // 2):
        lanes = slice(q * 128, (q + 1) * 128)
        xp = xs[:, lanes]
        parts = []
        for h in (2 * q, 2 * q + 1):
            across = cum2_rows[h : h + 1, :]
            down = cum2[:, h : h + 1]
            top = jnp.exp2(jnp.minimum(across[:, :half] - down[:half], 0.0)) * affinity[:half, :half]
            low = jnp.exp2(jnp.minimum(across - down[half:], 0.0)) * affinity[half:, :]
            parts.append(
                jnp.concatenate([dot(top.astype(BF16), xp[:half]), dot(low.astype(BF16), xp)], axis=0)
            )
        mixed = jnp.where(low_lane, parts[0], parts[1]) + skip[:, lanes] * x[:, lanes]
        mixed = mixed + dot(c, st_ref[q]) * ec[:, lanes]
        z = z_ref[:, lanes].astype(F32)
        gated = mixed * (z / (1.0 + jnp.exp(-z)))
        g_ref[:, lanes] = gated.astype(BF16)
        squares = squares + gated * gated
    high, low = halves(squares)
    ones = jnp.ones((8, 128), BF16)
    ss_ref[...] = dot(ones, high, NT) + dot(ones, low, NT)


def norm_kernel(g_ref, ss_ref, gain_ref, out_ref):
    total = dot(ss_ref[...], jnp.ones((8, 128), F32), TN, precision=HIGH)
    scale = lax.rsqrt(total * (1.0 / (MIXER_HEADS * P_SIZE)) + 1e-05)
    for q in range(HEADS // 2):
        lanes = slice(q * 128, (q + 1) * 128)
        out_ref[:, lanes] = (g_ref[:, lanes].astype(F32) * scale * gain_ref[:, lanes]).astype(BF16)


ROWS = 8 * BLOCK
LIMIT = 2.0**100


def keys_of(kv_ref, first, count):
    return kv_ref[pl.ds(first, count), :BLOCK, :].reshape(count * BLOCK, DH)


def values_of(kv_ref, first, count):
    return kv_ref[pl.ds(first, count), BLOCK:, :].reshape(count * BLOCK, DH)


def add_keys(qs_ref, k, v, l_ref, acc_ref, seen=None):
    lane = lax.broadcasted_iota(jnp.int32, k.shape, 1)
    ones = jnp.where(lane < 3, 1.0, 0.0).astype(BF16)
    score = dot(qs_ref[...], jnp.concatenate([k, ones], axis=1), NT)
    weights = []
    for j in range(0, k.shape[0], 128):
        weight = jnp.exp2(score[:, j : j + 128] * SCALE)
        if seen is not None:
            weight = jnp.where(seen[:, j : j + 128], weight, 0.0)
        weights.append(weight)
    l_ref[...] += sum(weights[1:], weights[0])
    acc_ref[...] += dot(jnp.concatenate([w.astype(BF16) for w in weights], axis=1), v)


def add_blocks(qs_ref, kv_ref, count, l_ref, acc_ref):
    @pl.loop(0, count // 2)
    def _(i):
        add_keys(qs_ref, keys_of(kv_ref, 2 * i, 2), values_of(kv_ref, 2 * i, 2), l_ref, acc_ref)

    @pl.when(count % 2 == 1)
    def _():
        at = count - 1
        add_keys(qs_ref, keys_of(kv_ref, at, 1), values_of(kv_ref, at, 1), l_ref, acc_ref)


def careful(qs_ref, kv_ref, count, m_ref, l_ref, acc_ref, diagonal=None):
    @pl.loop(0, 8)
    def _(h):
        rows = pl.ds(pl.multiple_of(h * BLOCK, BLOCK), BLOCK)

        def one(k, v, seen):
            score = dot(qs_ref[rows, :DH], k, NT) * SCALE
            if seen is not None:
                score = jnp.where(seen, score, -1e30)
            m_old = m_ref[rows, :]
            m_new = jnp.maximum(m_old, jnp.max(score, axis=1, keepdims=True))
            weight = jnp.exp2(score - m_new[:, :1])
            shrink = jnp.exp2(m_old - m_new)
            l_ref[rows, :] = l_ref[rows, :] * shrink + (weight[:, :128] + weight[:, 128:])
            acc_ref[rows, :] = acc_ref[rows, :] * shrink + dot(weight.astype(BF16), v)
            m_ref[rows, :] = m_new

        if diagonal is not None:
            one(*diagonal)

        @pl.loop(0, count)
        def _(b):
            one(keys_of(kv_ref, b, 1), values_of(kv_ref, b, 1), None)


def first_kernel(q_ref, own_ref, qs_ref, l_ref, acc_ref, tok_ref):
    tok_ref[...] = jnp.zeros((8, 128), F32)
    k = own_ref[:BLOCK, :]
    key = k.astype(F32)
    lane = lax.broadcasted_iota(jnp.int32, (BLOCK, DH), 1)
    for h in range(8):
        rows = slice(h * BLOCK, (h + 1) * BLOCK)
        q = q_ref[:, h * DH : (h + 1) * DH]
        qs_ref[rows, :DH] = q
        rest = -jnp.broadcast_to(jnp.sum(q.astype(F32) * key, axis=1, keepdims=True), (BLOCK, DH))
        pieces = jnp.zeros((BLOCK, DH), F32)
        for i in range(3):
            piece = rest.astype(BF16).astype(F32)
            pieces = jnp.where(lane == i, piece, pieces)
            rest = rest - piece
        qs_ref[rows, DH:] = pieces.astype(BF16)
    l_ref[...] = jnp.zeros((ROWS, DH), F32)
    acc_ref[...] = jnp.zeros((ROWS, DH), F32)
    row = lax.broadcasted_iota(jnp.int32, (ROWS, BLOCK), 0) & (BLOCK - 1)
    col = lax.broadcasted_iota(jnp.int32, (ROWS, BLOCK), 1)
    add_keys(qs_ref, k, own_ref[BLOCK:, :], l_ref, acc_ref, col <= row)


def next_kernel(n, counts_ref, qs_ref, *refs):
    kv_refs, (_, _, l_ref, acc_ref, tok_ref) = refs[:n], refs[n:]
    tok_ref[...] = jnp.zeros((8, 128), F32)
    for i, kv_ref in enumerate(kv_refs):
        add_blocks(qs_ref, kv_ref, counts_ref[i], l_ref, acc_ref)


def last_kernel(
    n, counts_ref, qs_ref, right_ref, left_ref, l_in, acc_in, own_ref, *refs
):
    kv_refs, (out_ref, l_ref, acc_ref, m_ref, kv_ref, held_ref, sem) = refs[:n], refs[n:]
    add_blocks(qs_ref, right_ref, counts_ref[n], l_ref, acc_ref)
    add_blocks(qs_ref, left_ref, counts_ref[n + 1], l_ref, acc_ref)

    @pl.when(jnp.logical_not(jnp.max(l_ref[...]) <= LIMIT))
    def _():
        l_ref[...] = jnp.zeros((ROWS, DH), F32)
        acc_ref[...] = jnp.zeros((ROWS, DH), F32)
        m_ref[...] = jnp.full((ROWS, DH), -1e30, F32)
        row = lax.broadcasted_iota(jnp.int32, (BLOCK, BLOCK), 0)
        col = lax.broadcasted_iota(jnp.int32, (BLOCK, BLOCK), 1)
        copy = pltpu.make_async_copy(own_ref, held_ref, sem)
        copy.start()
        copy.wait()
        own = (held_ref[:BLOCK, :], held_ref[BLOCK:, :], col <= row)
        for i in range(n):
            copy = pltpu.make_async_copy(kv_refs[i], kv_ref, sem)
            copy.start()
            copy.wait()
            diagonal = own if i == 0 else None
            careful(qs_ref, kv_ref, counts_ref[i], m_ref, l_ref, acc_ref, diagonal)
        careful(qs_ref, right_ref, counts_ref[n], m_ref, l_ref, acc_ref)
        careful(qs_ref, left_ref, counts_ref[n + 1], m_ref, l_ref, acc_ref)

    for h in range(8):
        rows = slice(h * BLOCK, (h + 1) * BLOCK)
        total = jnp.sum(l_ref[rows, :], axis=1, keepdims=True)
        out_ref[:, h * DH : (h + 1) * DH] = (acc_ref[rows, :] / total).astype(BF16)


SUMS = pltpu.VMEM((ROWS, DH), F32)
TOKEN = jax.ShapeDtypeStruct((8, 128), F32)
SMEM = pl.BlockSpec(memory_space=pltpu.SMEM)
VMEM = pl.BlockSpec(memory_space=pltpu.VMEM)
PLAIN = pl.BlockSpec()
ANY = pl.BlockSpec(memory_space=pl.ANY)
KERNEL = pltpu.CompilerParams(vmem_limit_bytes=28 * 2**20)


def cost_of(blocks):
    work = blocks * ROWS * BLOCK
    return pl.CostEstimate(flops=4 * work * DH, bytes_accessed=2**20, transcendentals=work)


def attend_first(queries, own):
    return pl.pallas_call(
        first_kernel,
        in_specs=[PLAIN, PLAIN],
        out_specs=[VMEM] * 3 + [PLAIN],
        out_shape=[pltpu.VMEM((ROWS, 2 * DH), BF16), SUMS, SUMS, TOKEN],
        compiler_params=KERNEL,
        cost_estimate=cost_of(1),
        name="attend_first",
    )(queries, own)


def attend_next(counts, stacked, kvs, sums):
    n = len(kvs)
    return pl.pallas_call(
        functools.partial(next_kernel, n),
        in_specs=[SMEM, VMEM] + [PLAIN] * n + [VMEM] * 2,
        out_specs=[VMEM] * 2 + [PLAIN],
        out_shape=[SUMS, SUMS, TOKEN],
        input_output_aliases={n + 2: 0, n + 3: 1},
        compiler_params=KERNEL,
        cost_estimate=cost_of(sum(kv.shape[0] for kv in kvs)),
        name="attend_next",
    )(counts, stacked, *kvs, *sums[:2])


def attend_last(counts, stacked, right, left, sums, own, kvs):
    return pl.pallas_call(
        functools.partial(last_kernel, len(kvs)),
        in_specs=[SMEM, VMEM, PLAIN, PLAIN, VMEM, VMEM, ANY] + [ANY] * len(kvs),
        out_specs=[PLAIN, VMEM, VMEM],
        out_shape=[jax.ShapeDtypeStruct((BLOCK, 8 * DH), BF16), SUMS, SUMS],
        scratch_shapes=[
            pltpu.VMEM((ROWS, DH), F32),
            pltpu.VMEM((XS, 2 * BLOCK, DH), BF16),
            pltpu.VMEM((2 * BLOCK, DH), BF16),
            pltpu.SemaphoreType.DMA,
        ],
        input_output_aliases={4: 1, 5: 2},
        compiler_params=KERNEL,
        cost_estimate=cost_of(4),
        name="attend_last",
    )(counts, stacked, right, left, *sums[:2], own, *kvs)[0]


def column_kernel(x_ref, own_ref, one_ref, two_ref, three_ref, tok_ref, out_ref):
    x = x_ref[0]
    for d, ref in enumerate((own_ref, one_ref, two_ref, three_ref)):
        out_ref[lax.rem(x + XS - d, XS)] = ref[...]


def halve_kernel(right_ref, left_ref, low_ref, high_ref):
    low_ref[...] = right_ref[: XS // 2]
    high_ref[...] = left_ref[XS // 2 :]


def spec_of(arg):
    if arg.dtype == jnp.int32:
        return SMEM
    return ANY if arg.shape == TOKEN.shape else PLAIN


def call(kernel, outs, cost, *args, limit=28, held=()):
    sources = [args[i] for i in held]
    scratch = [pltpu.VMEM(arg.shape, arg.dtype) for arg in sources]
    return pl.pallas_call(
        kernel,
        in_specs=[ANY if i in held else spec_of(arg) for i, arg in enumerate(args)],
        scratch_shapes=scratch + [pltpu.SemaphoreType.DMA((len(held),))] if held else [],
        out_shape=outs,
        compiler_params=pltpu.CompilerParams(vmem_limit_bytes=limit * 2**20),
        cost_estimate=pl.CostEstimate(flops=cost, bytes_accessed=3 * 2**20, transcendentals=2**20),
    )(*args)


def z_pairs(d):
    return [(x * ZS + z, x * ZS + (z + d) % ZS) for x in range(XS) for z in range(ZS)]


def x_pairs(d):
    return [(x * ZS + z, (x + d) % XS * ZS + z) for x in range(XS) for z in range(ZS)]


def z_send(a, d):
    return lax.ppermute(a, "ctx", z_pairs(d))


def x_send(a, d):
    return lax.ppermute(a, "ctx", x_pairs(d))


def per_device(
    ssm_input,
    gate_input,
    in_state,
    out_state,
    step_size,
    log_decay,
    skip_gain,
    norm_gain,
    queries,
    keys,
    values,
):
    place = lax.axis_index("ctx")
    x, z = place // ZS, place % ZS

    def visible(d, low=0, high=XS):
        other = (z + d) % ZS
        return jnp.clip(x + (other < z), low, high) - low

    whole = [jnp.stack([visible(-i), visible(i)]).astype(jnp.int32) for i in (1, 2, 3)]
    tail = jnp.stack([visible(4, 0, 2), visible(4, 2, 4)]).astype(jnp.int32)
    here = x.astype(jnp.int32).reshape(1)
    struct = jax.ShapeDtypeStruct

    own = jnp.concatenate([keys, values], axis=0)
    around = x_send(own, 1), x_send(own, 2), x_send(own, -1)
    stacked, *sums = attend_first(queries, own)
    step, decay = step_size.T, log_decay.T
    msg = call(
        contrib_kernel,
        struct((CTX, 48, 128), BF16),
        100_000_000,
        ssm_input,
        in_state,
        step,
        decay,
        sums[2],
        limit=46,
    )
    column = call(
        column_kernel, struct((XS, 2 * BLOCK, DH), BF16), 1_000_000, here, own, *around, sums[1]
    )
    right1, left1 = z_send(column, 1), z_send(column, -1)
    msg = lax.all_to_all(msg, "ctx", 0, 0)
    right2, left2 = z_send(right1, 1), z_send(left1, -1)
    counts = jnp.concatenate([here, whole[0]])
    sums = attend_next(counts, stacked, (column, right1, left1), sums)
    state = call(scan_kernel, struct((CTX, 32, 128), BF16), 1_000_000, msg, sums[2])
    state = lax.all_to_all(state, "ctx", 0, 0)
    right3, left3 = z_send(right2, 1), z_send(left2, -1)
    sums = attend_next(whole[1], stacked, (right2, left2), sums)
    gated, squares = call(
        mix_kernel,
        [struct((BLOCK, WIDTH), BF16), struct((8, BLOCK), F32)],
        500_000_000,
        ssm_input,
        in_state,
        out_state,
        step,
        decay,
        gate_input,
        skip_gain.reshape(1, HEADS),
        state.reshape(8, 128, 128),
        sums[2],
        limit=62,
        held=(0, 5, 7),
    )
    squares = lax.all_gather(squares[0], "head")
    half = struct((XS // 2, 2 * BLOCK, DH), BF16)
    right4, left4 = call(halve_kernel, [half, half], 1_000_000, right3, left3)
    right4, left4 = z_send(right4, 1), z_send(left4, -1)
    sums = attend_next(whole[2], stacked, (right3, left3), sums)
    mamba_out = call(
        norm_kernel,
        struct((BLOCK, WIDTH), BF16),
        10_000_000,
        gated,
        squares,
        norm_gain.reshape(1, WIDTH),
        limit=46,
    )
    counts = jnp.concatenate([here, *whole, tail])
    kvs = [column, right1, left1, right2, left2, right3, left3]
    attention_out = attend_last(counts, stacked, right4, left4, sums, own, kvs)
    return mamba_out, attention_out


def solution(mesh):
    both = P("ctx", "head")
    return jax.shard_map(
        per_device,
        mesh=mesh,
        in_specs=(both,) * 6 + (P("head"), P("head")) + (both,) * 3,
        out_specs=(both, both),
        check_vma=False,
    )
```
